512 devices in a mesh: dp: 64 (over z, y_lo, core), own: 8 (over y_hi, x).
Axes of the slice: x: 4, y: 4 (y_hi: 2, y_lo: 2; y = y_hi * 2 + y_lo), z: 16, core: 2. Of those that a mesh axis runs over, the one named last changes fastest.
Arguments:
- activations: bfloat16 [32768, 1, 1024], P('dp', None, 'own'), may hold values from -16 to 16
- output_grads: bfloat16 [32768, 3, 1024], P('dp', None, 'own'), may hold values from -16 to 16
- old_factors: float32 [4, 1024, 1024], P(None, 'dp', 'own'), may hold values from -2 to 2
- inverses: bfloat16 [8, 1, 1024, 1024], P('own', None, 'dp'), may hold values from -0.5 to 2.5, as said below
- owners: int32 [4], replicated, may hold values from 0 to 7, as said below
Outputs:
- new_factors: float32 [4, 1024, 1024], P(None, 'dp', 'own')
- preconditioned: float32 [3, 1024, 1, 1024], P(None, 'dp', None, 'own')
The draws below stay inside these ranges and needn't reach their ends.
Inputs may be any that keep to these rules, and one draw needn't show every extreme that they name: `owners`: no owner is named by more than 1 block, and one owner by exactly 1. `inverses`: slot s of owner o holds the symmetric inverse block of the s-th block, in block order, that owners maps to o; slots that no block maps to are not read.
All inputs are finite; a program needn't handle non-finite values.
Results may differ from the reference program's by a relative error of at most 0.0013.
The reference program's roundings to bfloat16 on the way count: a program that leaves them out, or rounds other values in their place, can miss the bound.
Values may be sent and summed in bfloat16 or wider, within the bound.
A program may use at most 64 MiB of HBM per device.

```python
import math
import jax
import jax.numpy as jnp

BLK = 1024
NBA = 1
NBG = 3
NB = 4
MOSTB = 1
OWNERS = 8
TOKENS = 32768


def draw_inverses(key, part):
    key = jax.random.fold_in(key, 11)
    first_key, second_key = jax.random.split(key)
    noise = jnp.clip(jax.random.normal(first_key, (OWNERS, MOSTB, BLK, BLK), jnp.float32), -4.0, 4.0)
    symmetric = (noise + jnp.swapaxes(noise, 2, 3)) * (0.5 / math.sqrt(BLK))
    diagonal = jax.random.uniform(second_key, (OWNERS, MOSTB, BLK), jnp.float32, 0.5, 2.0)
    identity = jnp.eye(BLK, dtype=jnp.float32)
    return (symmetric + diagonal[..., None] * identity).astype(jnp.bfloat16)


def shuffle_order(key, count):
    scores = jax.random.randint(key, (count,), 0, 1 << 20, dtype=jnp.int32)
    distinct = scores * count + jnp.arange(count, dtype=jnp.int32)
    return jnp.argsort(distinct, stable=True).astype(jnp.int32)


def draw_owners(key, part):
    key = jax.random.fold_in(key, 5)
    first_key, second_key = jax.random.split(key)
    slot_total = OWNERS * MOSTB
    shuffled = shuffle_order(first_key, slot_total)
    heavy = shuffled[0] // MOSTB
    positions = jnp.arange(slot_total, dtype=jnp.int32)
    slot_owner = shuffled // MOSTB
    at_end = ((slot_owner == 0) | (slot_owner == OWNERS - 1)) & (shuffled % MOSTB == 0)
    sort_keys = jnp.where(at_end, positions, positions + slot_total)
    sort_keys = jnp.where(slot_owner == heavy, positions + 2 * slot_total, sort_keys)
    remaining = shuffled[jnp.argsort(sort_keys, stable=True)]
    heavy_slots = heavy * MOSTB + jnp.arange(MOSTB, dtype=jnp.int32)
    chosen_slots = jnp.concatenate([heavy_slots, remaining[:NB - MOSTB]])
    order = shuffle_order(second_key, NB)
    return (chosen_slots[order] // MOSTB).astype(jnp.int32)


def with_spikes(result, stream_key, source, target, parts, factor):
    def block_of(axis_at):
        return (jnp.arange(result.shape[axis_at]) // (result.shape[axis_at] // parts)).reshape((-1,) + (1,) * (result.ndim - 1 - axis_at))

    near = jax.random.permutation(stream_key, parts)[block_of(target)]
    other_side = (block_of(target) + parts // 2) % parts
    return jnp.where((block_of(source) == near) | (block_of(source) == other_side), factor * result, result)


def level_of(stream_key, shape, pieces, smallest, high):
    def one(dim, blocks):
        steps = jax.random.uniform(jax.random.fold_in(jax.random.fold_in(stream_key, 6), dim), (blocks,), jnp.float32, smallest / len(pieces), high / len(pieces))
        return jnp.repeat(jnp.exp(steps), shape[dim] // blocks).reshape((-1,) + (1,) * (len(shape) - dim - 1))

    factor_of = one(*pieces[0])
    for cut in pieces[1:]:
        factor_of = factor_of * one(*cut)
    return factor_of


def gaussian(rng, extent, deviation, most, cuts=(), held_as=jnp.bfloat16):
    array = jax.random.normal(rng, extent, jnp.float32) * deviation
    if len(cuts) > 0:
        array = level_of(rng, extent, cuts, -0.22, 0.18) * array
    return jnp.clip(array, min=-most, max=most).astype(held_as)


def noise_with(rng, extent, spread, bound, cuts, heavy, kind=jnp.bfloat16):
    entries = spread * jax.random.normal(rng, extent, jnp.float32)
    if cuts:
        entries = entries * level_of(rng, extent, cuts, -0.22, 0.18)
    return jnp.clip(with_spikes(entries, jax.random.fold_in(rng, 3), *heavy), -bound, bound).astype(kind)


def setup_inputs(seed: int = 0) -> dict:
    seeds = jax.random.split(jax.random.key(seed), 6)
    return {
        "activations": noise_with(seeds[0], (TOKENS, NBA, BLK), 1.0, 16.0, ((0, 64), (2, 8)), (0, 2, 64, 4.0)),
        "output_grads": noise_with(seeds[1], (TOKENS, NBG, BLK), 1.0, 16.0, ((0, 64), (2, 8)), (0, 2, 64, 4.0)),
        "old_factors": gaussian(seeds[2], (NB, BLK, BLK), 0.3, 2.0, ((1, 64), (2, 8)), jnp.float32),
        "inverses": draw_inverses(jax.random.fold_in(seeds[5], 71), 0),
        "owners": draw_owners(jax.random.fold_in(seeds[5], 71), 0),
    }


FACTOR_DECAY = 0.9


def reference(activations, output_grads, old_factors, inverses, owners):
    columns = jnp.concatenate([activations, output_grads], axis=1)
    block_count = columns.shape[1]
    positions = jnp.arange(block_count, dtype=jnp.int32)
    same_owner = owners[:, None] == owners[None, :]
    block_rank = jnp.sum((same_owner & (positions[None, :] < positions[:, None])).astype(jnp.int32), axis=1)
    factor_list = []
    scaled_list = []
    for block in range(block_count):
        column_block = columns[:, block, :]
        covariance = jnp.dot(column_block.T, column_block, preferred_element_type=jnp.float32)
        factor_list.append(FACTOR_DECAY * old_factors[block] + ((1.0 - FACTOR_DECAY) / TOKENS) * covariance)
        inverse_block = inverses[owners[block], block_rank[block]]
        scaled_list.append(jnp.dot(column_block, inverse_block, preferred_element_type=jnp.float32).astype(jnp.bfloat16))
    new_factors = jnp.stack(factor_list, axis=0)
    gradient_rows = []
    for grad_block in range(NBG):
        act_list = []
        for act_block in range(NBA):
            product = jnp.dot(scaled_list[NBA + grad_block].T, scaled_list[act_block], preferred_element_type=jnp.float32)
            act_list.append(product / TOKENS)
        gradient_rows.append(jnp.stack(act_list, axis=1))
    preconditioned = jnp.stack(gradient_rows, axis=0)
    return new_factors, preconditioned
```

```python
import functools

import jax
import jax.numpy as jnp
from jax import lax
from jax.experimental import pallas as pl
from jax.experimental.pallas import tpu as pltpu
from jax.sharding import PartitionSpec as P

MESH = pl.DeviceIdType.MESH
FACTOR_DECAY = 0.9
TOKENS = 32768
TOK = 512
NZ = 16
HALF = NZ // 2
PIECES = 4
Q = 2
PER = PIECES // Q
LANE = 128
ROWS = 16


def gram(lhs8, rhs4, part, j_base):
    rhs = jnp.concatenate([rhs4[j_base + j] for j in range(PIECES)], axis=1)

    def tile(i, _):
        lhs = jnp.concatenate([lhs8[2 * i], lhs8[2 * i + 1]], axis=1)
        out = lax.dot_general(lhs, rhs, (((0,), (0,)), ((), ())), preferred_element_type=jnp.float32)
        for j in range(PIECES):
            part[j, pl.ds(4 * i, 4)] = out[:, j * LANE:(j + 1) * LANE].reshape(4, 2, 2, ROWS, LANE)
        return 0

    lax.fori_loop(0, 4, tile, 0)


def kernel(
    act, grads, old, inv, owners, nf_out, pr_out,
    cols, x8, shard, full_inv, s8, a4,
    part_c, part_p, half_c, half_p, right_c, right_p, left_c, left_p,
    ysum_c, ysum_p, yrecv_c, yrecv_p, fin_c, fin_p, frecv_c, frecv_p,
    loc_sem, xs_sem, xr_sem, is_sem, ir_sem, ns_sem, nr_sem, gs_sem, gr_sem,
    ss_sem, sr_sem, as_sem, ar_sem, cs_sem, cr_sem, rs_sem, rr_sem, ls_sem, lr_sem,
    ys_sem, yr_sem, fs_sem, fr_sem,
):
    dp = lax.axis_index("dp")
    own = lax.axis_index("own")
    z = dp // 4
    y = (dp // 2) % 2
    c = dp % 2
    h = own // 4
    x = own % 4

    def at(zz, yy, cc):
        return ((zz * 2 + yy) * 2 + cc, own)

    def member(hh, xx):
        return (dp, hh * 4 + xx)

    up = at((z + 1) % NZ, y, c)
    down = at((z + NZ - 1) % NZ, y, c)
    core = at(z, y, 1 - c)
    across = at(z, 1 - y, c)
    diagonal = at(z, 1 - y, 1 - c)
    peers = [((h + d // 4) % 2, (x + d % 4) % 4) for d in range(8)]

    loc = [
        pltpu.make_async_copy(act, cols.at[pl.ds(0, 1)], loc_sem.at[0]),
        pltpu.make_async_copy(grads, cols.at[pl.ds(1, 3)], loc_sem.at[1]),
        pltpu.make_async_copy(inv.at[:, pl.ds(h * 512, 512)], shard.at[own], loc_sem.at[2]),
    ]
    for copy in loc:
        copy.start()

    barrier = pltpu.get_barrier_semaphore()
    targets = [member(*peers[d]) for d in range(1, 8)] + [up, down, core, across, diagonal]
    for target in targets:
        pl.semaphore_signal(barrier, inc=1, device_id=target, device_id_type=MESH)
    pl.semaphore_wait(barrier, len(targets))

    sends = []

    def send(src, dst, s_sem, r_sem, target):
        copy = pltpu.make_async_remote_copy(
            src_ref=src, dst_ref=dst, send_sem=s_sem, recv_sem=r_sem, device_id=target, device_id_type=MESH
        )
        copy.start()
        return copy

    inv_copies = []
    for d in range(1, 8):
        hh, xx = peers[d]
        inv_copies.append(
            send(inv.at[:, pl.ds(hh * 512, 512)], shard.at[own], is_sem.at[d], ir_sem.at[d], member(hh, xx))
        )
    loc[0].wait()
    loc[1].wait()
    x_copies = []
    for d in range(1, 8):
        hh, xx = peers[d]
        x_copies.append(send(cols.at[xx], x8.at[own], xs_sem.at[d], xr_sem.at[d], member(hh, xx)))
    x8[own] = cols[x]
    loc[2].wait()

    for copy in inv_copies:
        copy.wait_recv()
    full_inv[dp] = shard[owners[x]]
    near = [
        send(full_inv.at[dp], full_inv.at[dp], ns_sem.at[k], nr_sem.at[k], target)
        for k, target in enumerate((core, across, diagonal))
    ]
    for copy in near:
        copy.wait_recv()

    def block(zz):
        return full_inv.at[pl.ds(((zz + NZ) % NZ) * 4, 4)]

    def gather_copy(s, right):
        zz = z - s if right else z + s
        k = s if right else HALF + s
        return pltpu.make_async_remote_copy(
            src_ref=block(zz), dst_ref=block(zz), send_sem=gs_sem.at[k], recv_sem=gr_sem.at[k],
            device_id=up if right else down, device_id_type=MESH,
        )

    for s in range(HALF):
        if s > 0:
            gather_copy(s - 1, True).wait_recv()
        gather_copy(s, True).start()
        if s < HALF - 1:
            if s > 0:
                gather_copy(s - 1, False).wait_recv()
            gather_copy(s, False).start()

    for copy in x_copies:
        copy.wait_recv()
    gram(x8, x8, part_c, h * PIECES)

    def order(k):
        if k == 15:
            return z
        return (z + HALF - k // 2) % NZ if k % 2 == 0 else (z + NZ - HALF + 1 + k // 2) % NZ

    def core_copy(n, part, half, k):
        t = order(k)
        return pltpu.make_async_remote_copy(
            src_ref=part.at[:, t, :, 1 - c], dst_ref=half.at[:, t],
            send_sem=cs_sem.at[n, k], recv_sem=cr_sem.at[n, k], device_id=core, device_id_type=MESH,
        )

    for k in range(16):
        core_copy(0, part_c, half_c, k).start()

    gather_copy(HALF - 1, True).wait_recv()
    gather_copy(HALF - 2, False).wait_recv()

    weights = full_inv[...].reshape(1024, 512)

    def scale_tile(i, _):
        rows = pl.ds(pl.multiple_of(i * 256, 256), 256)
        lhs = jnp.concatenate([x8[k, rows, :] for k in range(8)], axis=1)
        out = jnp.dot(lhs, weights, preferred_element_type=jnp.float32).astype(jnp.bfloat16)
        for j in range(PIECES):
            s8[h * PIECES + j, rows, :] = out[:, j * LANE:(j + 1) * LANE]
        return 0

    lax.fori_loop(0, TOK // 256, scale_tile, 0)

    mine = s8.at[pl.ds(h * PIECES, PIECES)]
    theirs = s8.at[pl.ds((1 - h) * PIECES, PIECES)]

    def swap_copy():
        return pltpu.make_async_remote_copy(
            src_ref=mine, dst_ref=mine, send_sem=ss_sem.at[0], recv_sem=sr_sem.at[0],
            device_id=member(1 - h, x), device_id_type=MESH,
        )

    def act_copy(g):
        return pltpu.make_async_remote_copy(
            src_ref=mine, dst_ref=a4, send_sem=as_sem.at[g], recv_sem=ar_sem.at[0],
            device_id=member(h, g), device_id_type=MESH,
        )

    @pl.when(x == 0)
    def _():
        for g in (1, 2, 3):
            act_copy(g).start()

    @pl.when(x > 0)
    def _():
        swap_copy().start()

    def reduce_scatter(n, part, half, right, left, ysum, yrecv, fin):
        def own_rows(t, js):
            return part[js, t, :, c] + half[js, t]

        def ring_copy(s, q, is_right):
            buf = right if is_right else left
            sem, rsem = (rs_sem, rr_sem) if is_right else (ls_sem, lr_sem)
            js = pl.ds(q * PER, PER)
            return pltpu.make_async_remote_copy(
                src_ref=buf.at[s, js], dst_ref=buf.at[s + 1, js],
                send_sem=sem.at[n, s, q], recv_sem=rsem.at[n, s, q],
                device_id=up if is_right else down, device_id_type=MESH,
            )

        for s in range(HALF):
            for is_right in (True, False):
                if not is_right and s == HALF - 1:
                    continue
                k = 2 * s if is_right else 2 * s + 1
                buf = right if is_right else left
                core_copy(n, part, half, k).wait_recv()
                for q in range(Q):
                    js = pl.ds(q * PER, PER)
                    term = own_rows(order(k), js)
                    if s > 0:
                        ring_copy(s - 1, q, is_right).wait_recv()
                        term = term + buf[s, js]
                    buf[s, js] = term
                    ring_copy(s, q, is_right).start()
        core_copy(n, part, half, 15).wait_recv()
        for q in range(Q):
            js = pl.ds(q * PER, PER)
            ring_copy(HALF - 1, q, True).wait_recv()
            ring_copy(HALF - 2, q, False).wait_recv()
            ysum[js] = own_rows(z, js) + right[HALF, js] + left[HALF - 1, js]
        cross = pltpu.make_async_remote_copy(
            src_ref=ysum.at[:, 1 - y], dst_ref=yrecv, send_sem=ys_sem.at[n], recv_sem=yr_sem.at[n],
            device_id=across, device_id_type=MESH,
        )
        cross.start()
        cross.wait_recv()
        fin[...] = ysum[:, y] + yrecv[...]
        for k in range(16):
            core_copy(n, part, half, k).wait_send()
        for s in range(HALF):
            for q in range(Q):
                ring_copy(s, q, True).wait_send()
                if s < HALF - 1:
                    ring_copy(s, q, False).wait_send()
        cross.wait_send()

    def final_copy(n, d, fin, frecv):
        xx = (x + d) % 4
        return pltpu.make_async_remote_copy(
            src_ref=fin.at[xx], dst_ref=frecv.at[x], send_sem=fs_sem.at[n, d], recv_sem=fr_sem.at[n, d],
            device_id=member(h, xx), device_id_type=MESH,
        )

    reduce_scatter(0, part_c, half_c, right_c, left_c, ysum_c, yrecv_c, fin_c)
    for d in (1, 2, 3):
        final_copy(0, d, fin_c, frecv_c).start()
    frecv_c[x] = fin_c[x]

    @pl.when(x == 0)
    def _():
        for g in (1, 2, 3):
            act_copy(g).wait_send()

    @pl.when(x > 0)
    def _():
        act_copy(0).wait_recv()
        swap_copy().wait_recv()
        gram(s8, a4, part_p, 0)
        for k in range(16):
            core_copy(1, part_p, half_p, k).start()
        reduce_scatter(1, part_p, half_p, right_p, left_p, ysum_p, yrecv_p, fin_p)
        for d in (1, 2, 3):
            final_copy(1, d, fin_p, frecv_p).start()
        frecv_p[x] = fin_p[x]
        swap_copy().wait_send()

    for d in (1, 2, 3):
        final_copy(0, d, fin_c, frecv_c).wait_recv()
    nf_out[...] = FACTOR_DECAY * old[...] + ((1.0 - FACTOR_DECAY) / TOKENS) * frecv_c[...]

    for d in (1, 2, 3):
        @pl.when((x + 4 - d) % 4 > 0)
        def _():
            final_copy(1, d, fin_p, frecv_p).wait_recv()
    pr_out[...] = frecv_p[1:4] * (1.0 / TOKENS)

    for copy in inv_copies + x_copies + near:
        copy.wait_send()
    for s in range(HALF):
        gather_copy(s, True).wait_send()
        if s < HALF - 1:
            gather_copy(s, False).wait_send()
    for d in (1, 2, 3):
        final_copy(0, d, fin_c, frecv_c).wait_send()

    @pl.when(x > 0)
    def _():
        for d in (1, 2, 3):
            final_copy(1, d, fin_p, frecv_p).wait_send()


def body(activations, output_grads, old_factors, inverses, owners):
    vmem = pl.BlockSpec(memory_space=pltpu.VMEM)
    hbm = pl.BlockSpec(memory_space=pl.ANY)
    bf16, f32 = jnp.bfloat16, jnp.float32
    twice = lambda shape: [pltpu.VMEM(shape, f32)] * 2
    dma = lambda *shape: pltpu.SemaphoreType.DMA(shape)
    new_factors, preconditioned = pl.pallas_call(
        kernel,
        out_shape=(
            jax.ShapeDtypeStruct((4, ROWS, LANE), f32),
            jax.ShapeDtypeStruct((3, ROWS, LANE), f32),
        ),
        in_specs=[hbm, hbm, vmem, hbm, pl.BlockSpec(memory_space=pltpu.SMEM)],
        out_specs=(vmem, vmem),
        scratch_shapes=[
            pltpu.VMEM((4, TOK, LANE), bf16),
            pltpu.VMEM((8, TOK, LANE), bf16),
            pltpu.VMEM((8, ROWS, 512), bf16),
            pltpu.VMEM((64, ROWS, 512), bf16),
            pltpu.VMEM((8, TOK, LANE), bf16),
            pltpu.VMEM((4, TOK, LANE), bf16),
            *twice((PIECES, NZ, 2, 2, ROWS, LANE)),
            *twice((PIECES, NZ, 2, ROWS, LANE)),
            *twice((HALF + 1, PIECES, 2, ROWS, LANE)),
            *twice((HALF, PIECES, 2, ROWS, LANE)),
            *twice((PIECES, 2, ROWS, LANE)),
            *twice((PIECES, ROWS, LANE)),
            *twice((PIECES, ROWS, LANE)),
            *twice((PIECES, ROWS, LANE)),
            dma(3),
            dma(8), dma(8), dma(8), dma(8), dma(3), dma(3), dma(16), dma(16),
            dma(1), dma(1), dma(4), dma(1), dma(2, 16), dma(2, 16),
            dma(2, HALF, Q), dma(2, HALF, Q), dma(2, HALF, Q), dma(2, HALF, Q),
            dma(2), dma(2), dma(2, 4), dma(2, 4),
        ],
        compiler_params=pltpu.CompilerParams(
            collective_id=0, has_side_effects=True, vmem_limit_bytes=40 * 1024 * 1024
        ),
    )(
        jnp.swapaxes(activations, 0, 1),
        jnp.swapaxes(output_grads, 0, 1),
        old_factors,
        inverses.reshape(ROWS, 1024),
        owners,
    )
    return new_factors, preconditioned.reshape(3, ROWS, 1, LANE)


def solution(mesh):
    placed = (
        P("dp", None, "own"),
        P("dp", None, "own"),
        P(None, "dp", "own"),
        P("own", None, "dp", None),
        P(),
    )
    return jax.shard_map(
        body,
        mesh=mesh,
        in_specs=placed,
        out_specs=(P(None, "dp", "own"), P(None, "dp", None, "own")),
        check_vma=False,
    )
```

```python
import jax
import jax.numpy as jnp
from jax import lax
from jax.experimental import pallas as pl
from jax.experimental.pallas import tpu as pltpu
from jax.sharding import PartitionSpec as P

MESH = pl.DeviceIdType.MESH
FACTOR_DECAY = 0.9
TOKENS = 32768
TOK = 512
PIECES = 4
LANE = 128
ROWS = 16


def gram(lhs8, rhs4, part, j_base):
    rhs = jnp.concatenate([rhs4[j_base + j] for j in range(PIECES)], axis=1)

    def tile(i, _):
        lhs = jnp.concatenate([lhs8[2 * i], lhs8[2 * i + 1]], axis=1)
        out = lax.dot_general(lhs, rhs, (((0,), (0,)), ((), ())), preferred_element_type=jnp.float32)
        for j in range(PIECES):
            part[j, i] = out[:, j * LANE:(j + 1) * LANE].reshape(4, 2, 2, ROWS, LANE)
        return 0

    lax.fori_loop(0, 4, tile, 0)


def kernel(
    act, grads, old, inv, owners, nf_out, pr_out,
    cols, x8, shard, full_inv, s8, a4, old_v,
    part, half, y_out, y_in, mid, near_in, far_out, far_in, fin, frecv,
    loc_sem, xs_sem, xr_sem, is_sem, ir_sem, ns_sem, nr_sem, fs_sem, fr_sem, as_sem, ar_sem, ps_sem, pr_sem,
    ss_sem, sr_sem, bs_sem, br_sem, cs_sem, cr_sem, ys_sem, yr_sem, zs_sem, zr_sem, ws_sem, wr_sem, ts_sem, tr_sem,
):
    dp = lax.axis_index("dp")
    own = lax.axis_index("own")
    z = dp // 4
    k = z // 4
    r = z % 4
    y = (dp // 2) % 2
    c = dp % 2
    h = own // 4
    x = own % 4

    def at(zz, yy, cc):
        return (((zz % 16) * 2 + yy) * 2 + cc, own)

    def member(hh, xx):
        return (dp, hh * 4 + xx)

    core = at(z, y, 1 - c)
    across = at(z, 1 - y, c)
    diagonal = at(z, 1 - y, 1 - c)
    by_z = {d: at(z + d, y, c) for d in (1, 15, 2, 14)}
    far = {d: at(((k + d) % 4) * 4 + r, y, c) for d in (1, 2, 3)}
    peers = [((h + d // 4) % 2, (x + d % 4) % 4) for d in range(8)]

    loc = [
        pltpu.make_async_copy(act, cols.at[pl.ds(0, 1)], loc_sem.at[0]),
        pltpu.make_async_copy(grads, cols.at[pl.ds(1, 3)], loc_sem.at[1]),
        pltpu.make_async_copy(inv.at[:, pl.ds(h * 512, 512)], shard.at[own], loc_sem.at[2]),
        pltpu.make_async_copy(old, old_v, loc_sem.at[3]),
    ]
    for copy in loc:
        copy.start()

    barrier = pltpu.get_barrier_semaphore()
    targets = [member(*peers[d]) for d in range(1, 8)] + [core, across, diagonal]
    targets = targets + list(by_z.values()) + list(far.values())
    for target in targets:
        pl.semaphore_signal(barrier, inc=1, device_id=target, device_id_type=MESH)
    pl.semaphore_wait(barrier, len(targets))

    def remote(src, dst, s_sem, r_sem, target):
        return pltpu.make_async_remote_copy(
            src_ref=src, dst_ref=dst, send_sem=s_sem, recv_sem=r_sem, device_id=target, device_id_type=MESH
        )

    def start(copies):
        for copy in copies:
            copy.start()
        return copies

    inv_copies = start([
        remote(inv.at[:, pl.ds(peers[d][0] * 512, 512)], shard.at[own], is_sem.at[d], ir_sem.at[d], member(*peers[d]))
        for d in (4, 1, 3, 5, 7, 2, 6)
    ])
    loc[0].wait()
    loc[1].wait()
    x_copies = start([
        remote(cols.at[peers[d][1]], x8.at[own], xs_sem.at[d], xr_sem.at[d], member(*peers[d]))
        for d in (4, 1, 6, 3, 5, 2, 7)
    ])
    x8[own] = cols[x]
    loc[2].wait()

    for copy in inv_copies:
        copy.wait_recv()
    full_inv[k, r, y, c] = shard[owners[x]]
    here = full_inv.at[k, r, y, c]
    near_copies = start([
        remote(here, here, ns_sem.at[i], nr_sem.at[i], target) for i, target in enumerate((core, across, diagonal))
    ])
    for copy in near_copies:
        copy.wait_recv()
    here = full_inv.at[k, r, c]
    far_copies = start([remote(here, here, fs_sem.at[d], fr_sem.at[d], far[d]) for d in (2, 1, 3)])

    def pass_copy(i, view):
        return remote(view, view, ps_sem.at[i], pr_sem.at[i], core)

    pass_copies = []
    get_copies = []

    def pass_on(i, view, other):
        pass_copies.append(pass_copy(i, view))
        pass_copies[-1].start()
        get_copies.append(pass_copy(i, other))

    for copy in x_copies:
        copy.wait_recv()
    gram(x8, x8, part.at[0], h * PIECES)

    def core_copy(n, j):
        return remote(part.at[n, j, :, :, :, 1 - c], half.at[n, j], cs_sem.at[n, j], cr_sem.at[n, j], core)

    def y_copy(n, j):
        return remote(y_out.at[n, j], y_in.at[n, j], ys_sem.at[n, j], yr_sem.at[n, j], across)

    def z_copies(n, j):
        two = 2 if j % 2 == 0 else 14
        return [
            remote(mid.at[n, j, :, (r + d) % 4], near_in.at[n, j, i], zs_sem.at[n, j, i], zr_sem.at[n, j, i], by_z[d])
            for i, d in enumerate((two, 1, 15))
        ]

    def w_copies(n, j):
        return [
            remote(far_out.at[n, j, (k + d) % 4], far_in.at[n, j, d - 1], ws_sem.at[n, j, d - 1],
                   wr_sem.at[n, j, d - 1], far[d])
            for d in (2, 1, 3)
        ]

    def final_copy(n, j):
        return remote(fin.at[n, j], frecv.at[n, x], ts_sem.at[n, j], tr_sem.at[n, x], member(h, j))

    def core_start(n):
        for j in range(PIECES):
            core_copy(n, j).start()

    def y_start(n, j):
        core_copy(n, j).wait_recv()
        y_out[n, j] = part[n, j, :, :, 1 - y, c] + half[n, j, :, :, 1 - y]
        y_copy(n, j).start()

    def z_start(n, j):
        y_copy(n, j).wait_recv()
        mid[n, j] = part[n, j, :, :, y, c] + half[n, j, :, :, y] + y_in[n, j]
        start(z_copies(n, j))

    def w_start(n, j):
        for copy in z_copies(n, j):
            copy.wait_recv()
        far_out[n, j] = mid[n, j, :, r] + near_in[n, j, 0] + near_in[n, j, 1] + near_in[n, j, 2]
        start(w_copies(n, j))

    def final_start(n, j):
        for copy in w_copies(n, j):
            copy.wait_recv()
        fin[n, j] = far_out[n, j, k] + far_in[n, j, 0] + far_in[n, j, 1] + far_in[n, j, 2]

        @pl.when(x != j)
        def _():
            final_copy(n, j).start()

        @pl.when(x == j)
        def _():
            frecv[n, j] = fin[n, j]

    def final_wait(n, xx):
        remote(fin.at[n, 0], frecv.at[n, xx], ts_sem.at[n, 0], tr_sem.at[n, xx], member(h, xx)).wait_recv()

    def drain(n):
        for j in range(PIECES):
            core_copy(n, j).wait_send()
            y_copy(n, j).wait_send()
            for copy in z_copies(n, j) + w_copies(n, j):
                copy.wait_send()

            @pl.when(x != j)
            def _():
                final_copy(n, j).wait_send()

    core_start(0)

    for i, (copy, d) in enumerate(zip(far_copies, (2, 1, 3))):
        copy.wait_recv()
    adj_copies = start([
        remote(full_inv.at[pl.ds(0, 2), r, c], full_inv.at[pl.ds(0, 2), r, c], as_sem.at[0], ar_sem.at[0], by_z[2]),
        remote(full_inv.at[pl.ds(2, 2), r, c], full_inv.at[pl.ds(2, 2), r, c], as_sem.at[1], ar_sem.at[1], by_z[14]),
        remote(full_inv.at[:, r, c], full_inv.at[:, r, c], as_sem.at[2], ar_sem.at[2], by_z[1]),
        remote(full_inv.at[:, r, c], full_inv.at[:, r, c], as_sem.at[3], ar_sem.at[3], by_z[15]),
    ])
    for d in (1, 2, 3):
        pass_on(d - 1, full_inv.at[(k + d) % 4, r, c], full_inv.at[(k + d) % 4, r, 1 - c])
    for j in range(PIECES):
        y_start(0, j)
    for i, (ks, d) in enumerate(((pl.ds(0, 4), 3), (pl.ds(0, 4), 1), (pl.ds(0, 2), 2), (pl.ds(2, 2), 2))):
        adj_copies[(2, 3, 0, 1)[i]].wait_recv()
        pass_on(3 + i, full_inv.at[ks, (r + d) % 4, c], full_inv.at[ks, (r + d) % 4, 1 - c])
    for copy in get_copies:
        copy.wait_recv()

    weights = full_inv[...].reshape(1024, 512)

    def scale_tile(i, _):
        rows = pl.ds(pl.multiple_of(i * 256, 256), 256)
        lhs = jnp.concatenate([x8[m, rows, :] for m in range(8)], axis=1)
        out = jnp.dot(lhs, weights, preferred_element_type=jnp.float32).astype(jnp.bfloat16)
        for j in range(PIECES):
            s8[h * PIECES + j, rows, :] = out[:, j * LANE:(j + 1) * LANE]
        return 0

    lax.fori_loop(0, TOK // 256, scale_tile, 0)

    mine = s8.at[pl.ds(h * PIECES, PIECES)]
    swap_copy = remote(mine, mine, ss_sem.at[0], sr_sem.at[0], member(1 - h, x))
    act_copies = [remote(mine, a4, bs_sem.at[g], br_sem.at[0], member(h, g)) for g in range(4)]

    @pl.when(x == 0)
    def _():
        for g in (2, 1, 3):
            act_copies[g].start()

    @pl.when(x > 0)
    def _():
        swap_copy.start()

    for j in range(PIECES):
        z_start(0, j)

    @pl.when(x > 0)
    def _():
        act_copies[0].wait_recv()
        swap_copy.wait_recv()
        gram(s8, a4, part.at[1], 0)
        core_start(1)

    for j in range(PIECES):
        w_start(0, j)

    @pl.when(x > 0)
    def _():
        for j in range(PIECES):
            y_start(1, j)

    for j in range(PIECES):
        final_start(0, j)

    @pl.when(x > 0)
    def _():
        for j in range(PIECES + 1):
            if j < PIECES:
                z_start(1, j)
            if j > 0:
                w_start(1, j - 1)
        for j in range(PIECES):
            final_start(1, j)

    loc[3].wait()
    for d in (1, 2, 3):
        final_wait(0, (x + d) % 4)
    nf_out[...] = FACTOR_DECAY * old_v[...] + ((1.0 - FACTOR_DECAY) / TOKENS) * frecv[0]

    for d in (1, 2, 3):
        @pl.when((x + d) % 4 > 0)
        def _():
            final_wait(1, (x + d) % 4)
    pr_out[...] = frecv[1, 1:4] * (1.0 / TOKENS)

    for copy in inv_copies + x_copies + near_copies + far_copies + adj_copies + pass_copies:
        copy.wait_send()
    drain(0)

    @pl.when(x == 0)
    def _():
        for g in (1, 2, 3):
            act_copies[g].wait_send()

    @pl.when(x > 0)
    def _():
        swap_copy.wait_send()
        drain(1)


def body(activations, output_grads, old_factors, inverses, owners):
    vmem = pl.BlockSpec(memory_space=pltpu.VMEM)
    hbm = pl.BlockSpec(memory_space=pl.ANY)
    bf16, f32 = jnp.bfloat16, jnp.float32
    dma = lambda *shape: pltpu.SemaphoreType.DMA(shape)
    new_factors, preconditioned = pl.pallas_call(
        kernel,
        out_shape=(
            jax.ShapeDtypeStruct((4, ROWS, LANE), f32),
            jax.ShapeDtypeStruct((3, ROWS, LANE), f32),
        ),
        in_specs=[hbm, hbm, hbm, hbm, pl.BlockSpec(memory_space=pltpu.SMEM)],
        out_specs=(vmem, vmem),
        scratch_shapes=[
            pltpu.VMEM((4, TOK, LANE), bf16),
            pltpu.VMEM((8, TOK, LANE), bf16),
            pltpu.VMEM((8, ROWS, 512), bf16),
            pltpu.VMEM((4, 4, 2, 2, ROWS, 512), bf16),
            pltpu.VMEM((8, TOK, LANE), bf16),
            pltpu.VMEM((4, TOK, LANE), bf16),
            pltpu.VMEM((4, ROWS, LANE), f32),
            pltpu.VMEM((2, PIECES, 4, 4, 2, 2, ROWS, LANE), f32),
            pltpu.VMEM((2, PIECES, 4, 4, 2, ROWS, LANE), f32),
            pltpu.VMEM((2, PIECES, 4, 4, ROWS, LANE), f32),
            pltpu.VMEM((2, PIECES, 4, 4, ROWS, LANE), f32),
            pltpu.VMEM((2, PIECES, 4, 4, ROWS, LANE), f32),
            pltpu.VMEM((2, PIECES, 3, 4, ROWS, LANE), f32),
            pltpu.VMEM((2, PIECES, 4, ROWS, LANE), f32),
            pltpu.VMEM((2, PIECES, 3, ROWS, LANE), f32),
            pltpu.VMEM((2, PIECES, ROWS, LANE), f32),
            pltpu.VMEM((2, PIECES, ROWS, LANE), f32),
            dma(4),
            dma(8), dma(8), dma(8), dma(8), dma(3), dma(3), dma(4), dma(4), dma(4), dma(4), dma(7), dma(7),
            dma(1), dma(1), dma(4), dma(1), dma(2, 4), dma(2, 4), dma(2, 4), dma(2, 4),
            dma(2, 4, 3), dma(2, 4, 3), dma(2, 4, 3), dma(2, 4, 3), dma(2, 4), dma(2, 4),
        ],
        compiler_params=pltpu.CompilerParams(
            collective_id=0, has_side_effects=True, vmem_limit_bytes=56 * 1024 * 1024
        ),
    )(
        jnp.swapaxes(activations, 0, 1),
        jnp.swapaxes(output_grads, 0, 1),
        old_factors,
        inverses.reshape(ROWS, 1024),
        owners,
    )
    return new_factors, preconditioned.reshape(3, ROWS, 1, LANE)


def solution(mesh):
    placed = (
        P("dp", None, "own"),
        P("dp", None, "own"),
        P(None, "dp", "own"),
        P("own", None, "dp", None),
        P(),
    )
    return jax.shard_map(
        body,
        mesh=mesh,
        in_specs=placed,
        out_specs=(P(None, "dp", "own"), P(None, "dp", None, "own")),
        check_vma=False,
    )
```

```python
import jax
import jax.numpy as jnp
from jax import lax
from jax.experimental import pallas as pl
from jax.experimental.pallas import tpu as pltpu
from jax.sharding import PartitionSpec as P

MESH = pl.DeviceIdType.MESH
FACTOR_DECAY = 0.9
TOKENS = 32768
TOK = 512
PIECES = 4
LANE = 128
ROWS = 16


def gram(lhs8, rhs4, part, j_base):
    rhs = jnp.concatenate([rhs4[j_base + j] for j in range(PIECES)], axis=1)

    def tile(i, _):
        lhs = jnp.concatenate([lhs8[2 * i], lhs8[2 * i + 1]], axis=1)
        out = lax.dot_general(lhs, rhs, (((0,), (0,)), ((), ())), preferred_element_type=jnp.float32)
        for j in range(PIECES):
            part[j, i] = out[:, j * LANE:(j + 1) * LANE].reshape(4, 2, 2, ROWS, LANE)
        return 0

    lax.fori_loop(0, 4, tile, 0)


def kernel(
    act, grads, old, inv, owners, nf_out, pr_out,
    cols, x8, shard, full_inv, s8, a4, old_v, part, half,
    mid_c, near_c, out_c, in_c, sum_c, cross_c,
    y_out, y_in, mid_p, near_p, out_p, in_p,
    loc_sem, xs_sem, xr_sem, is_sem, ir_sem, ns_sem, nr_sem, fs_sem, fr_sem, as_sem, ar_sem, ps_sem, pr_sem,
    ss_sem, sr_sem, bs_sem, br_sem, cs_sem, cr_sem, ys_sem, yr_sem, zs_sem, zr_sem, ws_sem, wr_sem, ts_sem, tr_sem,
):
    dp = lax.axis_index("dp")
    own = lax.axis_index("own")
    z = dp // 4
    k = z // 4
    r = z % 4
    y = (dp // 2) % 2
    c = dp % 2
    h = own // 4
    x = own % 4

    def at(zz, yy, cc, mm):
        return (((zz % 16) * 2 + yy) * 2 + cc, mm)

    def member(hh, xx):
        return (dp, hh * 4 + xx)

    def far(d, xx):
        return at(((k + d) % 4) * 4 + r, y, c, h * 4 + xx)

    core = at(z, y, 1 - c, own)
    across = at(z, 1 - y, c, own)
    diagonal = at(z, 1 - y, 1 - c, own)
    by_z = {d: at(z + d, y, c, own) for d in (1, 15, 2, 14)}
    peers = [((h + d // 4) % 2, (x + d % 4) % 4) for d in range(8)]

    loc = [
        pltpu.make_async_copy(act, cols.at[pl.ds(0, 1)], loc_sem.at[0]),
        pltpu.make_async_copy(grads, cols.at[pl.ds(1, 3)], loc_sem.at[1]),
        pltpu.make_async_copy(inv.at[:, pl.ds(h * 512, 512)], shard.at[own], loc_sem.at[2]),
        pltpu.make_async_copy(old, old_v, loc_sem.at[3]),
    ]
    for copy in loc:
        copy.start()

    barrier = pltpu.get_barrier_semaphore()
    targets = [far(d, (x + e) % 4) for d in (2, 1, 3) for e in range(4)] + list(by_z.values())
    targets = targets + [member(*peers[d]) for d in range(1, 8)] + [core, across, diagonal]
    for target in targets:
        pl.semaphore_signal(barrier, inc=1, device_id=target, device_id_type=MESH)
    pl.semaphore_wait(barrier, len(targets))

    def remote(src, dst, s_sem, r_sem, target):
        return pltpu.make_async_remote_copy(
            src_ref=src, dst_ref=dst, send_sem=s_sem, recv_sem=r_sem, device_id=target, device_id_type=MESH
        )

    def start(copies):
        for copy in copies:
            copy.start()
        return copies

    inv_copies = start([
        remote(inv.at[:, pl.ds(peers[d][0] * 512, 512)], shard.at[own], is_sem.at[d], ir_sem.at[d], member(*peers[d]))
        for d in (4, 1, 3, 5, 7, 2, 6)
    ])
    loc[2].wait()
    for copy in inv_copies:
        copy.wait_recv()

    mine = shard[owners[x]]
    for u in range(2):
        full_inv[u, k, r, y, c] = mine[:, u * 256:(u + 1) * 256]
    here = full_inv.at[:, k, r, y, c]
    near_copies = start([
        remote(here, here, ns_sem.at[i], nr_sem.at[i], target) for i, target in enumerate((across, diagonal, core))
    ])

    loc[0].wait()
    loc[1].wait()
    x_copies = start([
        remote(cols.at[peers[d][1]], x8.at[own], xs_sem.at[d], xr_sem.at[d], member(*peers[d]))
        for d in (4, 1, 6, 3, 5, 2, 7)
    ])
    x8[own] = cols[x]

    for copy in near_copies:
        copy.wait_recv()

    def far_copy(u, d):
        view = full_inv.at[u, k, r, c]
        return remote(view, view, fs_sem.at[u, d], fr_sem.at[u, d], far(d, x))

    def adj_copy(u, i):
        view = (full_inv.at[u, pl.ds(0, 2), r, c], full_inv.at[u, pl.ds(2, 2), r, c], full_inv.at[u, :, r, c],
                full_inv.at[u, :, r, c])[i]
        return remote(view, view, as_sem.at[u, i], ar_sem.at[u, i], by_z[(2, 14, 1, 15)[i]])

    def pass_views(u, cc):
        views = [full_inv.at[u, (k + d) % 4, r, cc] for d in (1, 2, 3)]
        return views + [
            full_inv.at[u, pl.ds(0, 2), (r + 2) % 4, cc], full_inv.at[u, pl.ds(2, 2), (r + 2) % 4, cc],
            full_inv.at[u, :, (r + 3) % 4, cc], full_inv.at[u, :, (r + 1) % 4, cc],
        ]

    def pass_copy(u, i, cc):
        view = pass_views(u, cc)[i]
        return remote(view, view, ps_sem.at[u, i], pr_sem.at[u, i], core)

    for u in range(2):
        for d in (2, 1, 3):
            far_copy(u, d).start()
    for u in range(2):
        for d in (2, 1, 3):
            far_copy(u, d).wait_recv()
        for i in range(4):
            adj_copy(u, i).start()
        for i in range(3):
            pass_copy(u, i, c).start()

    for copy in x_copies:
        copy.wait_recv()
    gram(x8, x8, part.at[0], h * PIECES)

    def core_copy(n, j):
        return remote(part.at[n, j, :, :, :, 1 - c], half.at[n, j], cs_sem.at[n, j], cr_sem.at[n, j], core)

    for j in range(PIECES):
        core_copy(0, j).start()

    def scale(u):
        for i in range(4):
            adj_copy(u, i).wait_recv()
            pass_copy(u, 3 + i, c).start()
        for i in range(7):
            pass_copy(u, i, 1 - c).wait_recv()
        weights = full_inv[u].reshape(1024, 256)

        def tile(i, _):
            rows = pl.ds(pl.multiple_of(i * 256, 256), 256)
            lhs = jnp.concatenate([x8[m, rows, :] for m in range(8)], axis=1)
            out = jnp.dot(lhs, weights, preferred_element_type=jnp.float32).astype(jnp.bfloat16)
            for j in range(2):
                s8[h * PIECES + 2 * u + j, rows, :] = out[:, j * LANE:(j + 1) * LANE]
            return 0

        lax.fori_loop(0, TOK // 256, tile, 0)

    def swap_copy(u):
        view = s8.at[pl.ds(h * PIECES + 2 * u, 2)]
        return remote(view, view, ss_sem.at[u], sr_sem.at[u], member(1 - h, x))

    def act_copy(j, g):
        return remote(s8.at[h * PIECES + j], a4.at[j], bs_sem.at[j, g // 2], br_sem.at[j], member(h, g))

    def hand_copy(j):
        return remote(a4.at[j], a4.at[j], bs_sem.at[j, 0], br_sem.at[j], member(h, 2))

    def scaled_start(u):
        @pl.when(x == 0)
        def _():
            for i in range(2):
                act_copy(2 * u + i, 1).start()
                act_copy(2 * u + 1 - i, 3).start()

        @pl.when(x > 0)
        def _():
            swap_copy(u).start()

    def hand_on(u):
        for i, g in enumerate((1, 3)):
            @pl.when(x == g)
            def _():
                hand_copy(2 * u + i).wait_recv()
                hand_copy(2 * u + i).start()

    def two_away(j):
        return 2 if j % 2 == 0 else 14

    def near_c_copies(j):
        return [
            remote(mid_c.at[j, :, (r + d) % 4], near_c.at[j, i], zs_sem.at[0, j, i], zr_sem.at[0, j, i], by_z[d])
            for i, d in enumerate((two_away(j), 1, 15))
        ]

    def near_c_start(j):
        core_copy(0, j).wait_recv()
        mid_c[j] = part[0, j, :, :, :, c] + half[0, j]
        start(near_c_copies(j))

    def out_copy(n, out, dst, j, d):
        return remote(out.at[j, (k + d) % 4], dst.at[x, d], ws_sem.at[n, j, d], wr_sem.at[n, x, d], far(d, j))

    def out_start(n, out, dst, j):
        for d in (2, 1, 3):
            out_copy(n, out, dst, j, d).start()

        @pl.when(x != j)
        def _():
            out_copy(n, out, dst, j, 0).start()

        @pl.when(x == j)
        def _():
            dst[j, 0] = out[j, k]

    def out_wait(n, out, dst, xx):
        def arrived(d):
            remote(out.at[0, 0], dst.at[xx, d], ws_sem.at[n, 0, d], wr_sem.at[n, xx, d], far(d, xx)).wait_recv()

        for d in (1, 2, 3):
            arrived(d)

        @pl.when(x != xx)
        def _():
            arrived(0)

    def out_drain(n, out, dst):
        for j in range(PIECES):
            for d in (1, 2, 3):
                out_copy(n, out, dst, j, d).wait_send()

            @pl.when(x != j)
            def _():
                out_copy(n, out, dst, j, 0).wait_send()

    def out_c_start(j):
        for copy in near_c_copies(j):
            copy.wait_recv()
        out_c[j] = mid_c[j, :, r] + near_c[j, 0] + near_c[j, 1] + near_c[j, 2]
        out_start(0, out_c, in_c, j)

    cross_copy = remote(sum_c.at[:, 1 - y], cross_c, ts_sem.at[0], tr_sem.at[0], across)

    def y_copy(j):
        return remote(y_out.at[j], y_in.at[j], ys_sem.at[j], yr_sem.at[j], across)

    def near_p_copies(j):
        return [
            remote(mid_p.at[j, :, (r + d) % 4], near_p.at[j, i], zs_sem.at[1, j, i], zr_sem.at[1, j, i], by_z[d])
            for i, d in enumerate((two_away(j), 1, 15))
        ]

    def y_start(j):
        core_copy(1, j).wait_recv()
        y_out[j] = part[1, j, :, :, 1 - y, c] + half[1, j, :, :, 1 - y]
        y_copy(j).start()

    def near_p_start(j):
        y_copy(j).wait_recv()
        mid_p[j] = part[1, j, :, :, y, c] + half[1, j, :, :, y] + y_in[j]
        start(near_p_copies(j))

    def out_p_start(j):
        for copy in near_p_copies(j):
            copy.wait_recv()
        out_p[j] = mid_p[j, :, r] + near_p[j, 0] + near_p[j, 1] + near_p[j, 2]
        out_start(1, out_p, in_p, j)

    scale(0)
    scaled_start(0)
    scale(1)
    scaled_start(1)
    for j in range(PIECES):
        near_c_start(j)
    hand_on(0)
    hand_on(1)
    for j in range(2):
        out_c_start(j)

    @pl.when(x > 0)
    def _():
        for u in range(2):
            swap_copy(u).wait_recv()
            for i, g in enumerate((1, 3)):
                @pl.when(x != g)
                def _():
                    act_copy(2 * u + i, 1).wait_recv()
        gram(s8, a4, part.at[1], 0)
        for j in range(PIECES):
            core_copy(1, j).start()
        for j in range(PIECES):
            y_start(j)

    for j in range(2, PIECES):
        out_c_start(j)

    @pl.when(x > 0)
    def _():
        near_p_start(0)

    for xx in range(PIECES):
        out_wait(0, out_c, in_c, xx)
        sum_c[xx] = in_c[xx, 0] + in_c[xx, 1] + in_c[xx, 2] + in_c[xx, 3]
    cross_copy.start()

    @pl.when(x > 0)
    def _():
        for j in range(1, PIECES + 1):
            if j < PIECES:
                near_p_start(j)
            out_p_start(j - 1)

    cross_copy.wait_recv()
    loc[3].wait()
    total = sum_c[:, y] + cross_c[...]
    nf_out[...] = FACTOR_DECAY * old_v[...] + ((1.0 - FACTOR_DECAY) / TOKENS) * total

    for xx in range(1, PIECES):
        out_wait(1, out_p, in_p, xx)
        pr_out[xx - 1] = (in_p[xx, 0] + in_p[xx, 1] + in_p[xx, 2] + in_p[xx, 3]) * (1.0 / TOKENS)

    for copy in inv_copies + x_copies + near_copies + [cross_copy]:
        copy.wait_send()
    for u in range(2):
        for d in (1, 2, 3):
            far_copy(u, d).wait_send()
        for i in range(4):
            adj_copy(u, i).wait_send()
        for i in range(7):
            pass_copy(u, i, c).wait_send()
    for j in range(PIECES):
        core_copy(0, j).wait_send()
        for copy in near_c_copies(j):
            copy.wait_send()
    out_drain(0, out_c, in_c)

    @pl.when(x == 0)
    def _():
        for j in range(PIECES):
            act_copy(j, 1).wait_send()
            act_copy(j, 3).wait_send()

    for i, g in enumerate((1, 3)):
        @pl.when(x == g)
        def _():
            for u in range(2):
                hand_copy(2 * u + i).wait_send()

    @pl.when(x > 0)
    def _():
        for u in range(2):
            swap_copy(u).wait_send()
        for j in range(PIECES):
            core_copy(1, j).wait_send()
            y_copy(j).wait_send()
            for copy in near_p_copies(j):
                copy.wait_send()
        out_drain(1, out_p, in_p)


def body(activations, output_grads, old_factors, inverses, owners):
    vmem = pl.BlockSpec(memory_space=pltpu.VMEM)
    hbm = pl.BlockSpec(memory_space=pl.ANY)
    bf16, f32 = jnp.bfloat16, jnp.float32
    dma = lambda *shape: pltpu.SemaphoreType.DMA(shape)
    new_factors, preconditioned = pl.pallas_call(
        kernel,
        out_shape=(
            jax.ShapeDtypeStruct((4, ROWS, LANE), f32),
            jax.ShapeDtypeStruct((3, ROWS, LANE), f32),
        ),
        in_specs=[hbm, hbm, hbm, hbm, pl.BlockSpec(memory_space=pltpu.SMEM)],
        out_specs=(vmem, vmem),
        scratch_shapes=[
            pltpu.VMEM((4, TOK, LANE), bf16),
            pltpu.VMEM((8, TOK, LANE), bf16),
            pltpu.VMEM((8, ROWS, 512), bf16),
            pltpu.VMEM((2, 4, 4, 2, 2, ROWS, 256), bf16),
            pltpu.VMEM((8, TOK, LANE), bf16),
            pltpu.VMEM((4, TOK, LANE), bf16),
            pltpu.VMEM((4, ROWS, LANE), f32),
            pltpu.VMEM((2, PIECES, 4, 4, 2, 2, ROWS, LANE), f32),
            pltpu.VMEM((2, PIECES, 4, 4, 2, ROWS, LANE), f32),
            pltpu.VMEM((PIECES, 4, 4, 2, ROWS, LANE), f32),
            pltpu.VMEM((PIECES, 3, 4, 2, ROWS, LANE), f32),
            pltpu.VMEM((PIECES, 4, 2, ROWS, LANE), f32),
            pltpu.VMEM((PIECES, 4, 2, ROWS, LANE), f32),
            pltpu.VMEM((PIECES, 2, ROWS, LANE), f32),
            pltpu.VMEM((PIECES, ROWS, LANE), f32),
            pltpu.VMEM((PIECES, 4, 4, ROWS, LANE), f32),
            pltpu.VMEM((PIECES, 4, 4, ROWS, LANE), f32),
            pltpu.VMEM((PIECES, 4, 4, ROWS, LANE), f32),
            pltpu.VMEM((PIECES, 3, 4, ROWS, LANE), f32),
            pltpu.VMEM((PIECES, 4, ROWS, LANE), f32),
            pltpu.VMEM((PIECES, 4, ROWS, LANE), f32),
            dma(4),
            dma(8), dma(8), dma(8), dma(8), dma(3), dma(3), dma(2, 4), dma(2, 4), dma(2, 4), dma(2, 4), dma(2, 7),
            dma(2, 7), dma(2), dma(2), dma(4, 2), dma(4), dma(2, 4), dma(2, 4), dma(4), dma(4),
            dma(2, 4, 3), dma(2, 4, 3), dma(2, 4, 4), dma(2, 4, 4), dma(1), dma(1),
        ],
        compiler_params=pltpu.CompilerParams(
            collective_id=0, has_side_effects=True, vmem_limit_bytes=56 * 1024 * 1024
        ),
    )(
        jnp.swapaxes(activations, 0, 1),
        jnp.swapaxes(output_grads, 0, 1),
        old_factors,
        inverses.reshape(ROWS, 1024),
        owners,
    )
    return new_factors, preconditioned.reshape(3, ROWS, 1, LANE)


def solution(mesh):
    placed = (
        P("dp", None, "own"),
        P("dp", None, "own"),
        P(None, "dp", "own"),
        P("own", None, "dp", None),
        P(),
    )
    return jax.shard_map(
        body,
        mesh=mesh,
        in_specs=placed,
        out_specs=(P(None, "dp", "own"), P(None, "dp", None, "own")),
        check_vma=False,
    )
```

```python
import jax
import jax.numpy as jnp
from jax import lax
from jax.experimental import pallas as pl
from jax.experimental.pallas import tpu as pltpu
from jax.sharding import PartitionSpec as P

MESH = pl.DeviceIdType.MESH
FACTOR_DECAY = 0.9
TOKENS = 32768
TOK = 512
PIECES = 4
LANE = 128
ROWS = 16


def gram(lhs8, rhs4, part, j_base):
    rhs = jnp.concatenate([rhs4[j_base + j] for j in range(PIECES)], axis=1)

    def tile(i, _):
        lhs = jnp.concatenate([lhs8[2 * i], lhs8[2 * i + 1]], axis=1)
        out = lax.dot_general(lhs, rhs, (((0,), (0,)), ((), ())), preferred_element_type=jnp.float32)
        for j in range(PIECES):
            part[j, i] = out[:, j * LANE:(j + 1) * LANE].reshape(4, 2, 2, ROWS, LANE)
        return 0

    lax.fori_loop(0, 4, tile, 0)


def kernel(
    act, grads, old, inv, owners, nf_out, pr_out,
    cols, x8, shard, full_inv, s8, a4, old_v, part, half,
    mid_z, near_z, out_z, in_z, sum_z, cross_in,
    y_out, y_in, mid_y, near_y, out_y, in_y,
    loc_sem, xs_sem, xr_sem, is_sem, ir_sem, ns_sem, nr_sem, fs_sem, fr_sem, as_sem, ar_sem, ps_sem, pr_sem,
    ss_sem, sr_sem, bs_sem, br_sem, cs_sem, cr_sem, ys_sem, yr_sem, zs_sem, zr_sem, ws_sem, wr_sem, ts_sem, tr_sem,
    chain_2, chain_4,
):
    dp = lax.axis_index("dp")
    own = lax.axis_index("own")
    z = dp // 4
    k = z // 4
    r = z % 4
    y = (dp // 2) % 2
    c = dp % 2
    h = own // 4
    x = own % 4

    def at(zz, yy, cc, mm):
        return (((zz % 16) * 2 + yy) * 2 + cc, mm)

    def member(hh, xx):
        return (dp, hh * 4 + xx)

    def far(d, xx):
        return at(((k + d) % 4) * 4 + r, y, c, h * 4 + xx)

    core = at(z, y, 1 - c, own)
    across = at(z, 1 - y, c, own)
    diagonal = at(z, 1 - y, 1 - c, own)
    by_z = {d: at(z + d, y, c, own) for d in (1, 15, 2, 14)}
    peers = [((h + d // 4) % 2, (x + d % 4) % 4) for d in range(8)]

    loc = [
        pltpu.make_async_copy(act, cols.at[pl.ds(0, 1)], loc_sem.at[0]),
        pltpu.make_async_copy(grads, cols.at[pl.ds(1, 3)], loc_sem.at[1]),
        pltpu.make_async_copy(inv.at[:, pl.ds(h * 512, 512)], shard.at[own], loc_sem.at[2]),
        pltpu.make_async_copy(old, old_v, loc_sem.at[3]),
    ]
    for copy in loc:
        copy.start()

    barrier = pltpu.get_barrier_semaphore()
    targets = list(by_z.values()) + [member(*peers[d]) for d in range(1, 8)] + [core, across, diagonal]
    for target in targets:
        pl.semaphore_signal(barrier, inc=1, device_id=target, device_id_type=MESH)
    pl.semaphore_wait(barrier, len(targets))
    for d in (2, 14):
        pl.semaphore_signal(chain_2, inc=1, device_id=by_z[d], device_id_type=MESH)

    def remote(src, dst, s_sem, r_sem, target):
        return pltpu.make_async_remote_copy(
            src_ref=src, dst_ref=dst, send_sem=s_sem, recv_sem=r_sem, device_id=target, device_id_type=MESH
        )

    def start(copies):
        for copy in copies:
            copy.start()
        return copies

    inv_copies = start([
        remote(inv.at[:, pl.ds(peers[d][0] * 512, 512)], shard.at[own], is_sem.at[d], ir_sem.at[d], member(*peers[d]))
        for d in (4, 1, 3, 5, 7, 2, 6)
    ])
    pl.semaphore_wait(chain_2, 2)
    for d in (1, 3):
        pl.semaphore_signal(chain_4, inc=1, device_id=far(d, x), device_id_type=MESH)
    loc[2].wait()
    for copy in inv_copies:
        copy.wait_recv()

    mine = shard[owners[x]]
    for u in range(2):
        full_inv[u, k, r, y, c] = mine[:, u * 256:(u + 1) * 256]
    here = full_inv.at[:, k, r, y, c]
    near_copies = start([
        remote(here, here, ns_sem.at[i], nr_sem.at[i], target) for i, target in enumerate((across, diagonal, core))
    ])

    loc[0].wait()
    loc[1].wait()
    x_copies = start([
        remote(cols.at[peers[d][1]], x8.at[own], xs_sem.at[d], xr_sem.at[d], member(*peers[d]))
        for d in (4, 1, 6, 3, 5, 2, 7)
    ])
    x8[own] = cols[x]

    for copy in near_copies:
        copy.wait_recv()

    def far_copy(u, d):
        view = full_inv.at[u, k, r, c]
        return remote(view, view, fs_sem.at[u, d], fr_sem.at[u, d], far(d, x))

    def adj_copy(u, d, i):
        b = (k + d) % 4
        view = full_inv.at[u, b, r, c]
        if i < 2:
            target = by_z[(1, 15)[i]]
        else:
            target = at(z + 2 + (b // 2) * 12, y, c, own)
        return remote(view, view, as_sem.at[u, d, i], ar_sem.at[u, b, i], target)

    def adj_wait(u, i):
        for b in range(4):
            view = full_inv.at[u, b, (r + (3, 1, 2)[i]) % 4, c]
            remote(view, view, as_sem.at[u, 0, i], ar_sem.at[u, b, i], by_z[1]).wait_recv()

    def pass_views(u, cc):
        views = [full_inv.at[u, (k + d) % 4, r, cc] for d in (1, 2, 3)]
        return views + [
            full_inv.at[u, :, (r + 3) % 4, cc], full_inv.at[u, :, (r + 1) % 4, cc], full_inv.at[u, :, (r + 2) % 4, cc],
        ]

    def pass_copy(u, i, cc):
        view = pass_views(u, cc)[i]
        return remote(view, view, ps_sem.at[u, i], pr_sem.at[u, i], core)

    pl.semaphore_wait(chain_4, 2)
    for u in range(2):
        for d in (2, 1, 3):
            far_copy(u, d).start()
    for u in range(2):
        for i in range(3):
            adj_copy(u, 0, i).start()
    for d in (1, 3, 2):
        for u in range(2):
            far_copy(u, d).wait_recv()
            for i in range(3):
                adj_copy(u, 4 - d, i).start()
            pass_copy(u, 3 - d, c).start()

    for copy in x_copies:
        copy.wait_recv()
    gram(x8, x8, part.at[0], h * PIECES)

    def piece(i):
        return (x + i) % 4

    def core_copy(n, i):
        j = piece(i)
        return remote(part.at[n, j, :, :, :, 1 - c], half.at[n, j], cs_sem.at[n, i], cr_sem.at[n, i], core)

    for i in (3, 0, 1, 2):
        core_copy(0, i).start()

    def z_first(n, i):
        return n == 0 and i < 3

    def slot(n, i):
        return i if z_first(n, i) else i + 1 if n == 1 else 0

    def y_copy(n, i):
        q = slot(n, i)
        return remote(y_out.at[q], y_in.at[q], ys_sem.at[q], yr_sem.at[q], across)

    def y_start(n, i):
        j = piece(i)
        core_copy(n, i).wait_recv()
        y_out[slot(n, i)] = part[n, j, :, :, 1 - y, c] + half[n, j, :, :, 1 - y]
        if n == 1 and i > 0:
            y_copy(n, i - 1).wait_send()
        y_copy(n, i).start()

    y_start(0, 3)

    def scale(u):
        for i in range(3):
            adj_wait(u, i)
            pass_copy(u, 3 + i, c).start()
        for i in range(6):
            pass_copy(u, i, 1 - c).wait_recv()
        weights = full_inv[u].reshape(1024, 256)

        def tile(i, _):
            rows = pl.ds(pl.multiple_of(i * 256, 256), 256)
            lhs = jnp.concatenate([x8[m, rows, :] for m in range(8)], axis=1)
            out = jnp.dot(lhs, weights, preferred_element_type=jnp.float32).astype(jnp.bfloat16)
            for j in range(2):
                s8[h * PIECES + 2 * u + j, rows, :] = out[:, j * LANE:(j + 1) * LANE]
            return 0

        lax.fori_loop(0, TOK // 256, tile, 0)

    def swap_copy(u):
        view = s8.at[pl.ds(h * PIECES + 2 * u, 2)]
        return remote(view, view, ss_sem.at[u], sr_sem.at[u], member(1 - h, x))

    def act_copy(j, g):
        return remote(s8.at[h * PIECES + j], a4.at[j], bs_sem.at[j, g // 2], br_sem.at[j], member(h, g))

    def hand_copy(j):
        return remote(a4.at[j], a4.at[j], bs_sem.at[j, 0], br_sem.at[j], member(h, 2))

    def scaled_start(u):
        @pl.when(x == 0)
        def _():
            for i in range(2):
                act_copy(2 * u + i, 1).start()
                act_copy(2 * u + 1 - i, 3).start()

        @pl.when(x > 0)
        def _():
            swap_copy(u).start()

    def hand_on(u):
        for i, g in enumerate((1, 3)):
            @pl.when(x == g)
            def _():
                hand_copy(2 * u + i).wait_recv()
                hand_copy(2 * u + i).start()

    def buffers(n, i):
        return (mid_z, near_z, out_z, in_z) if z_first(n, i) else (mid_y, near_y, out_y, in_y)

    def near_copies_of(n, i):
        mid, near, _, _ = buffers(n, i)
        q = slot(n, i)
        return [
            remote(mid.at[q, :, (r + d) % 4], near.at[q, e], zs_sem.at[n, i, e], zr_sem.at[n, i, e], by_z[d])
            for e, d in enumerate((2 if i % 2 == 0 else 14, 1, 15))
        ]

    def near_start(n, i):
        j, q = piece(i), slot(n, i)
        if z_first(n, i):
            core_copy(n, i).wait_recv()
            mid_z[q] = part[n, j, :, :, :, c] + half[n, j]
            if i > 0:
                for copy in near_copies_of(n, i - 1):
                    copy.wait_send()
        else:
            y_copy(n, i).wait_recv()
            mid_y[q] = part[n, j, :, :, y, c] + half[n, j, :, :, y] + y_in[q]
        start(near_copies_of(n, i))

    def out_copy(n, i, d):
        _, _, out, into = buffers(n, i)
        q = slot(n, i)
        return remote(out.at[q, (k + d) % 4], into.at[q, d], ws_sem.at[n, i, d], wr_sem.at[n, i, d], far(d, piece(i)))

    def outs(i):
        return (2, 1, 3) if i == 0 else (2, 1, 3, 0)

    def out_start(n, i):
        mid, near, out, into = buffers(n, i)
        q = slot(n, i)
        for copy in near_copies_of(n, i):
            copy.wait_recv()
        out[q] = mid[q, :, r] + near[q, 0] + near[q, 1] + near[q, 2]
        for d in outs(i):
            out_copy(n, i, d).start()
        if i == 0:
            into[q, 0] = out[q, k]

    def arrived(n, i):
        into, q = buffers(n, i)[3], slot(n, i)
        for d in outs(i):
            out_copy(n, i, d).wait_recv()
        return into[q, 0] + into[q, 1] + into[q, 2] + into[q, 3]

    def source(i):
        return (x + 4 - i) % 4

    cross_copy = remote(sum_z.at[:, 1 - y], cross_in, ts_sem.at[0], tr_sem.at[0], across)

    def drain(n):
        for i in range(PIECES):
            core_copy(n, i).wait_send()
            for d in outs(i):
                out_copy(n, i, d).wait_send()
            if not (z_first(n, i) and i < 2):
                for copy in near_copies_of(n, i):
                    copy.wait_send()
        y_copy(n, 3).wait_send()

    scale(0)
    scaled_start(0)
    scale(1)
    scaled_start(1)
    near_start(0, 0)
    hand_on(0)
    near_start(0, 1)
    hand_on(1)
    near_start(0, 2)
    out_start(0, 0)
    near_start(0, 3)
    out_start(0, 1)

    @pl.when(x > 0)
    def _():
        for u in range(2):
            swap_copy(u).wait_recv()
            for i, g in enumerate((1, 3)):
                @pl.when(x != g)
                def _():
                    act_copy(2 * u + i, 1).wait_recv()
        gram(s8, a4, part.at[1], 0)
        core_copy(1, 0).start()
        core_copy(1, 1).start()
        y_start(1, 0)
        core_copy(1, 2).start()
        core_copy(1, 3).start()

    out_start(0, 2)

    @pl.when(x > 0)
    def _():
        y_start(1, 1)
        near_start(1, 0)

    out_start(0, 3)

    @pl.when(x > 0)
    def _():
        y_start(1, 2)
        near_start(1, 1)
        y_start(1, 3)
        out_start(1, 0)
        near_start(1, 2)
        out_start(1, 1)
        near_start(1, 3)
        out_start(1, 2)
        out_start(1, 3)

    for i in range(3):
        sum_z[i] = arrived(0, i)
    cross_copy.start()
    loc[3].wait()

    def factors(i, total):
        b = source(i)
        nf_out[b] = FACTOR_DECAY * old_v[b] + ((1.0 - FACTOR_DECAY) / TOKENS) * total

    factors(3, arrived(0, 3))
    cross_copy.wait_recv()
    for i in range(3):
        factors(i, sum_z[i, y] + cross_in[i])

    for i in range(PIECES):
        @pl.when(source(i) > 0)
        def _():
            pr_out[source(i) - 1] = arrived(1, i) * (1.0 / TOKENS)

    for copy in inv_copies + x_copies + near_copies + [cross_copy]:
        copy.wait_send()
    for u in range(2):
        for d in (1, 2, 3):
            far_copy(u, d).wait_send()
        for d in range(4):
            for i in range(3):
                adj_copy(u, d, i).wait_send()
        for i in range(6):
            pass_copy(u, i, c).wait_send()
    drain(0)

    @pl.when(x == 0)
    def _():
        for j in range(PIECES):
            act_copy(j, 1).wait_send()
            act_copy(j, 3).wait_send()

    for i, g in enumerate((1, 3)):
        @pl.when(x == g)
        def _():
            for u in range(2):
                hand_copy(2 * u + i).wait_send()

    @pl.when(x > 0)
    def _():
        for u in range(2):
            swap_copy(u).wait_send()
        drain(1)


def body(activations, output_grads, old_factors, inverses, owners):
    vmem = pl.BlockSpec(memory_space=pltpu.VMEM)
    hbm = pl.BlockSpec(memory_space=pl.ANY)
    bf16, f32 = jnp.bfloat16, jnp.float32
    dma = lambda *shape: pltpu.SemaphoreType.DMA(shape)
    new_factors, preconditioned = pl.pallas_call(
        kernel,
        out_shape=(
            jax.ShapeDtypeStruct((4, ROWS, LANE), f32),
            jax.ShapeDtypeStruct((3, ROWS, LANE), f32),
        ),
        in_specs=[hbm, hbm, hbm, hbm, pl.BlockSpec(memory_space=pltpu.SMEM)],
        out_specs=(vmem, vmem),
        scratch_shapes=[
            pltpu.VMEM((4, TOK, LANE), bf16),
            pltpu.VMEM((8, TOK, LANE), bf16),
            pltpu.VMEM((8, ROWS, 512), bf16),
            pltpu.VMEM((2, 4, 4, 2, 2, ROWS, 256), bf16),
            pltpu.VMEM((8, TOK, LANE), bf16),
            pltpu.VMEM((4, TOK, LANE), bf16),
            pltpu.VMEM((4, ROWS, LANE), f32),
            pltpu.VMEM((2, PIECES, 4, 4, 2, 2, ROWS, LANE), f32),
            pltpu.VMEM((2, PIECES, 4, 4, 2, ROWS, LANE), f32),
            pltpu.VMEM((3, 4, 4, 2, ROWS, LANE), f32),
            pltpu.VMEM((3, 3, 4, 2, ROWS, LANE), f32),
            pltpu.VMEM((3, 4, 2, ROWS, LANE), f32),
            pltpu.VMEM((3, 4, 2, ROWS, LANE), f32),
            pltpu.VMEM((3, 2, ROWS, LANE), f32),
            pltpu.VMEM((3, ROWS, LANE), f32),
            pltpu.VMEM((5, 4, 4, ROWS, LANE), f32),
            pltpu.VMEM((5, 4, 4, ROWS, LANE), f32),
            pltpu.VMEM((5, 4, 4, ROWS, LANE), f32),
            pltpu.VMEM((5, 3, 4, ROWS, LANE), f32),
            pltpu.VMEM((5, 4, ROWS, LANE), f32),
            pltpu.VMEM((5, 4, ROWS, LANE), f32),
            dma(4),
            dma(8), dma(8), dma(8), dma(8), dma(3), dma(3), dma(2, 4), dma(2, 4), dma(2, 4, 3), dma(2, 4, 3), dma(2, 6),
            dma(2, 6), dma(2), dma(2), dma(4, 2), dma(4), dma(2, 4), dma(2, 4), dma(5), dma(5),
            dma(2, 4, 3), dma(2, 4, 3), dma(2, 4, 4), dma(2, 4, 4), dma(1), dma(1),
            pltpu.SemaphoreType.REGULAR, pltpu.SemaphoreType.REGULAR,
        ],
        compiler_params=pltpu.CompilerParams(
            collective_id=0, has_side_effects=True, vmem_limit_bytes=60 * 1024 * 1024
        ),
    )(
        jnp.swapaxes(activations, 0, 1),
        jnp.swapaxes(output_grads, 0, 1),
        old_factors,
        inverses.reshape(ROWS, 1024),
        owners,
    )
    return new_factors, preconditioned.reshape(3, ROWS, 1, LANE)


def solution(mesh):
    placed = (
        P("dp", None, "own"),
        P("dp", None, "own"),
        P(None, "dp", "own"),
        P("own", None, "dp", None),
        P(),
    )
    return jax.shard_map(
        body,
        mesh=mesh,
        in_specs=placed,
        out_specs=(P(None, "dp", "own"), P(None, "dp", None, "own")),
        check_vma=False,
    )
```

```python
import jax
import jax.numpy as jnp
from jax import lax
from jax.experimental import pallas as pl
from jax.experimental.pallas import tpu as pltpu
from jax.sharding import PartitionSpec as P

MESH = pl.DeviceIdType.MESH
FACTOR_DECAY = 0.9
TOKENS = 32768
TOK = 512
PIECES = 4
LANE = 128
ROWS = 16


def gram(lhs8, rhs4, part, j_base, pieces):
    rhs = jnp.concatenate([rhs4[j_base + j] for j in pieces], axis=1)

    def tile(i, _):
        lhs = jnp.concatenate([lhs8[2 * i], lhs8[2 * i + 1]], axis=1)
        out = lax.dot_general(lhs, rhs, (((0,), (0,)), ((), ())), preferred_element_type=jnp.float32)
        for e, j in enumerate(pieces):
            part[j, i] = out[:, e * LANE:(e + 1) * LANE].reshape(4, 2, 2, ROWS, LANE)
        return 0

    lax.fori_loop(0, 4, tile, 0)


def kernel(
    act, grads, old, inv, owners, nf_out, pr_out,
    owner_s, cols, x8, shard, full_inv, s8, a4, old_v, part, half,
    mid_z, near_z, out_z, in_z, sum_z, cross_in,
    y_out, y_in, mid_y, near_y, out_y, in_y,
    loc_sem, xs_sem, xr_sem, is_sem, ir_sem, ns_sem, nr_sem, fs_sem, fr_sem, as_sem, ar_sem, ps_sem, pr_sem,
    ss_sem, sr_sem, bs_sem, br_sem, cs_sem, cr_sem, ys_sem, yr_sem, zs_sem, zr_sem, ws_sem, wr_sem, ts_sem, tr_sem,
    chain_2, chain_4,
):
    dp = lax.axis_index("dp")
    own = lax.axis_index("own")
    z = dp // 4
    k = z // 4
    r = z % 4
    y = (dp // 2) % 2
    c = dp % 2
    h = own // 4
    x = own % 4

    def at(zz, yy, cc, mm):
        return (((zz % 16) * 2 + yy) * 2 + cc, mm)

    def member(hh, xx):
        return (dp, hh * 4 + xx)

    def far(d, xx):
        return at(((k + d) % 4) * 4 + r, y, c, h * 4 + xx)

    core = at(z, y, 1 - c, own)
    across = at(z, 1 - y, c, own)
    diagonal = at(z, 1 - y, 1 - c, own)
    by_z = {d: at(z + d, y, c, own) for d in (1, 15, 2, 14)}
    peers = [((h + d // 4) % 2, (x + d % 4) % 4) for d in range(8)]

    loc = [
        pltpu.make_async_copy(act, cols.at[pl.ds(0, 1)], loc_sem.at[0]),
        pltpu.make_async_copy(grads, cols.at[pl.ds(1, 3)], loc_sem.at[1]),
        pltpu.make_async_copy(inv.at[:, pl.ds(h * 512, 512)], shard.at[own], loc_sem.at[2]),
        pltpu.make_async_copy(old, old_v, loc_sem.at[3]),
        pltpu.make_async_copy(owners, owner_s, loc_sem.at[4]),
    ]
    for copy in loc:
        copy.start()

    barrier = pltpu.get_barrier_semaphore()
    targets = list(by_z.values()) + [member(*peers[d]) for d in range(1, 8)] + [core, across, diagonal]
    for target in targets:
        pl.semaphore_signal(barrier, inc=1, device_id=target, device_id_type=MESH)
    pl.semaphore_wait(barrier, len(targets))
    for d in (2, 14):
        pl.semaphore_signal(chain_2, inc=1, device_id=by_z[d], device_id_type=MESH)

    def remote(src, dst, s_sem, r_sem, target):
        return pltpu.make_async_remote_copy(
            src_ref=src, dst_ref=dst, send_sem=s_sem, recv_sem=r_sem, device_id=target, device_id_type=MESH
        )

    def start(copies):
        for copy in copies:
            copy.start()
        return copies

    inv_copies = start([
        remote(inv.at[:, pl.ds(peers[d][0] * 512, 512)], shard.at[own], is_sem.at[d], ir_sem.at[d], member(*peers[d]))
        for d in (4, 1, 3, 5, 7, 2, 6)
    ])
    pl.semaphore_wait(chain_2, 2)
    for d in (1, 3):
        pl.semaphore_signal(chain_4, inc=1, device_id=far(d, x), device_id_type=MESH)
    loc[2].wait()
    loc[4].wait()
    for copy in inv_copies:
        copy.wait_recv()

    mine = shard[owner_s[x]]
    for u in range(2):
        full_inv[u, k, r, y, c] = mine[:, u * 256:(u + 1) * 256]
    here = full_inv.at[:, k, r, y, c]
    near_copies = start([
        remote(here, here, ns_sem.at[i], nr_sem.at[i], target) for i, target in enumerate((across, diagonal, core))
    ])

    loc[0].wait()
    loc[1].wait()
    x_copies = start([
        remote(cols.at[peers[d][1]], x8.at[own], xs_sem.at[d], xr_sem.at[d], member(*peers[d]))
        for d in (4, 1, 6, 3, 5, 2, 7)
    ])
    x8[own] = cols[x]

    for copy in near_copies:
        copy.wait_recv()

    def far_copy(u, d):
        view = full_inv.at[u, k, r, c]
        return remote(view, view, fs_sem.at[u, d], fr_sem.at[u, d], far(d, x))

    def adj_copy(u, d, i):
        b = (k + d) % 4
        view = full_inv.at[u, b, r, c]
        if i < 2:
            target = by_z[(1, 15)[i]]
        else:
            target = at(z + 2 + (b // 2) * 12, y, c, own)
        return remote(view, view, as_sem.at[u, d, i], ar_sem.at[u, b, i], target)

    def adj_wait(u, i):
        for b in range(4):
            view = full_inv.at[u, b, (r + (3, 1, 2)[i]) % 4, c]
            remote(view, view, as_sem.at[u, 0, i], ar_sem.at[u, b, i], by_z[1]).wait_recv()

    def pass_views(u, cc):
        views = [full_inv.at[u, (k + d) % 4, r, cc] for d in (1, 2, 3)]
        return views + [
            full_inv.at[u, :, (r + 3) % 4, cc], full_inv.at[u, :, (r + 1) % 4, cc], full_inv.at[u, :, (r + 2) % 4, cc],
        ]

    def pass_copy(u, i, cc):
        view = pass_views(u, cc)[i]
        return remote(view, view, ps_sem.at[u, i], pr_sem.at[u, i], core)

    pl.semaphore_wait(chain_4, 2)
    for u in range(2):
        for d in (2, 1, 3):
            far_copy(u, d).start()
    for u in range(2):
        for i in range(3):
            adj_copy(u, 0, i).start()
    for d in (1, 3, 2):
        for u in range(2):
            far_copy(u, d).wait_recv()
            for i in range(3):
                adj_copy(u, 4 - d, i).start()
            pass_copy(u, 3 - d, c).start()

    for copy in x_copies:
        copy.wait_recv()
    gram(x8, x8, part.at[0], h * PIECES, range(PIECES))

    def piece(i):
        return (x + i) % 4

    def core_copy(n, i):
        j = piece(i)
        return remote(part.at[n, j, :, :, :, 1 - c], half.at[n, j], cs_sem.at[n, i], cr_sem.at[n, i], core)

    for i in (3, 0, 1, 2):
        core_copy(0, i).start()

    def z_first(n, i):
        return n == 0 and i < 3

    def slot(n, i):
        return i if z_first(n, i) else i + 1 if n == 1 else 0

    def y_copy(n, i):
        q = slot(n, i)
        return remote(y_out.at[q], y_in.at[q], ys_sem.at[q], yr_sem.at[q], across)

    def y_start(n, i):
        j = piece(i)
        core_copy(n, i).wait_recv()
        y_out[slot(n, i)] = part[n, j, :, :, 1 - y, c] + half[n, j, :, :, 1 - y]
        if n == 1 and i > 1:
            y_copy(n, i - 2).wait_send()
        y_copy(n, i).start()

    y_start(0, 3)

    def scale(u):
        for i in range(3):
            adj_wait(u, i)
            pass_copy(u, 3 + i, c).start()
        for i in range(6):
            pass_copy(u, i, 1 - c).wait_recv()
        weights = full_inv[u].reshape(1024, 256)

        def tile(i, _):
            rows = pl.ds(pl.multiple_of(i * 256, 256), 256)
            lhs = jnp.concatenate([x8[m, rows, :] for m in range(8)], axis=1)
            out = jnp.dot(lhs, weights, preferred_element_type=jnp.float32).astype(jnp.bfloat16)
            for j in range(2):
                s8[h * PIECES + 2 * u + j, rows, :] = out[:, j * LANE:(j + 1) * LANE]
            return 0

        lax.fori_loop(0, TOK // 256, tile, 0)

    def swap_copy(u):
        view = s8.at[pl.ds(h * PIECES + 2 * u, 2)]
        return remote(view, view, ss_sem.at[u], sr_sem.at[u], member(1 - h, x))

    def act_copy(j, g):
        return remote(s8.at[h * PIECES + j], a4.at[j], bs_sem.at[j, g // 2], br_sem.at[j], member(h, g))

    def hand_copy(j):
        return remote(a4.at[j], a4.at[j], bs_sem.at[j, 0], br_sem.at[j], member(h, 2))

    def scaled_start(u):
        @pl.when(x == 0)
        def _():
            for i in range(2):
                act_copy(2 * u + i, 1).start()
                act_copy(2 * u + 1 - i, 3).start()

        @pl.when(x > 0)
        def _():
            swap_copy(u).start()

    def hand_on(u):
        for i, g in enumerate((1, 3)):
            @pl.when(x == g)
            def _():
                hand_copy(2 * u + i).wait_recv()
                hand_copy(2 * u + i).start()

    def buffers(n, i):
        return (mid_z, near_z, out_z, in_z) if z_first(n, i) else (mid_y, near_y, out_y, in_y)

    def near_copies_of(n, i):
        mid, near, _, _ = buffers(n, i)
        q = slot(n, i)
        return [
            remote(mid.at[q, :, (r + d) % 4], near.at[q, e], zs_sem.at[n, i, e], zr_sem.at[n, i, e], by_z[d])
            for e, d in enumerate((2 if i % 2 == 0 else 14, 1, 15))
        ]

    def near_start(n, i):
        j, q = piece(i), slot(n, i)
        if z_first(n, i):
            core_copy(n, i).wait_recv()
            mid_z[q] = part[n, j, :, :, :, c] + half[n, j]
        else:
            y_copy(n, i).wait_recv()
            mid_y[q] = part[n, j, :, :, y, c] + half[n, j, :, :, y] + y_in[q]
        start(near_copies_of(n, i))

    def out_copy(n, i, d):
        _, _, out, into = buffers(n, i)
        q = slot(n, i)
        return remote(out.at[q, (k + d) % 4], into.at[q, d], ws_sem.at[n, i, d], wr_sem.at[n, i, d], far(d, piece(i)))

    def outs(i):
        return (2, 1, 3) if i == 0 else (2, 1, 3, 0)

    def out_start(n, i):
        mid, near, out, into = buffers(n, i)
        q = slot(n, i)
        for copy in near_copies_of(n, i):
            copy.wait_recv()
        out[q] = mid[q, :, r] + near[q, 0] + near[q, 1] + near[q, 2]
        for d in outs(i):
            out_copy(n, i, d).start()
        if i == 0:
            into[q, 0] = out[q, k]

    def arrived(n, i):
        into, q = buffers(n, i)[3], slot(n, i)
        for d in outs(i):
            out_copy(n, i, d).wait_recv()
        return into[q, 0] + into[q, 1] + into[q, 2] + into[q, 3]

    def source(i):
        return (x + 4 - i) % 4

    cross_copy = remote(sum_z.at[:, 1 - y], cross_in, ts_sem.at[0], tr_sem.at[0], across)

    def drain(n):
        for i in range(PIECES):
            core_copy(n, i).wait_send()
            for d in outs(i):
                out_copy(n, i, d).wait_send()
            for copy in near_copies_of(n, i):
                copy.wait_send()
        for i in range(3 - n, 4):
            y_copy(n, i).wait_send()

    scale(0)
    scaled_start(0)
    near_start(0, 0)
    near_start(0, 1)
    scale(1)
    scaled_start(1)
    hand_on(0)
    hand_on(1)
    near_start(0, 2)
    out_start(0, 0)
    near_start(0, 3)
    out_start(0, 1)

    @pl.when(x > 0)
    def _():
        for u in range(2):
            swap_copy(u).wait_recv()
            for i, g in enumerate((1, 3)):
                @pl.when(x != g)
                def _():
                    act_copy(2 * u + i, 1).wait_recv()
        gram(s8, a4, part.at[1], 0, [piece(0), piece(1)])
        core_copy(1, 0).start()
        core_copy(1, 1).start()
        gram(s8, a4, part.at[1], 0, [piece(2), piece(3)])
        y_start(1, 0)
        core_copy(1, 2).start()
        core_copy(1, 3).start()

    out_start(0, 2)

    @pl.when(x > 0)
    def _():
        y_start(1, 1)
        near_start(1, 0)

    out_start(0, 3)

    @pl.when(x > 0)
    def _():
        y_start(1, 2)
        near_start(1, 1)
        y_start(1, 3)
        out_start(1, 0)
        near_start(1, 2)
        out_start(1, 1)
        near_start(1, 3)
        out_start(1, 2)
        out_start(1, 3)

    for i in range(3):
        sum_z[i] = arrived(0, i)
    cross_copy.start()
    loc[3].wait()

    def factors(i, total):
        b = source(i)
        nf_out[b] = FACTOR_DECAY * old_v[b] + ((1.0 - FACTOR_DECAY) / TOKENS) * total

    factors(3, arrived(0, 3))
    cross_copy.wait_recv()
    for i in range(3):
        factors(i, sum_z[i, y] + cross_in[i])

    for i in range(PIECES):
        @pl.when(source(i) > 0)
        def _():
            pr_out[source(i) - 1] = arrived(1, i) * (1.0 / TOKENS)

    for copy in inv_copies + x_copies + near_copies + [cross_copy]:
        copy.wait_send()
    for u in range(2):
        for d in (1, 2, 3):
            far_copy(u, d).wait_send()
        for d in range(4):
            for i in range(3):
                adj_copy(u, d, i).wait_send()
        for i in range(6):
            pass_copy(u, i, c).wait_send()
    drain(0)

    @pl.when(x == 0)
    def _():
        for j in range(PIECES):
            act_copy(j, 1).wait_send()
            act_copy(j, 3).wait_send()

    for i, g in enumerate((1, 3)):
        @pl.when(x == g)
        def _():
            for u in range(2):
                hand_copy(2 * u + i).wait_send()

    @pl.when(x > 0)
    def _():
        for u in range(2):
            swap_copy(u).wait_send()
        drain(1)


def body(activations, output_grads, old_factors, inverses, owners):
    vmem = pl.BlockSpec(memory_space=pltpu.VMEM)
    hbm = pl.BlockSpec(memory_space=pl.ANY)
    bf16, f32 = jnp.bfloat16, jnp.float32
    dma = lambda *shape: pltpu.SemaphoreType.DMA(shape)
    new_factors, preconditioned = pl.pallas_call(
        kernel,
        out_shape=(
            jax.ShapeDtypeStruct((4, ROWS, LANE), f32),
            jax.ShapeDtypeStruct((3, ROWS, LANE), f32),
        ),
        in_specs=[hbm, hbm, hbm, hbm, hbm],
        out_specs=(vmem, vmem),
        scratch_shapes=[
            pltpu.SMEM((4,), jnp.int32),
            pltpu.VMEM((4, TOK, LANE), bf16),
            pltpu.VMEM((8, TOK, LANE), bf16),
            pltpu.VMEM((8, ROWS, 512), bf16),
            pltpu.VMEM((2, 4, 4, 2, 2, ROWS, 256), bf16),
            pltpu.VMEM((8, TOK, LANE), bf16),
            pltpu.VMEM((4, TOK, LANE), bf16),
            pltpu.VMEM((4, ROWS, LANE), f32),
            pltpu.VMEM((2, PIECES, 4, 4, 2, 2, ROWS, LANE), f32),
            pltpu.VMEM((2, PIECES, 4, 4, 2, ROWS, LANE), f32),
            pltpu.VMEM((3, 4, 4, 2, ROWS, LANE), f32),
            pltpu.VMEM((3, 3, 4, 2, ROWS, LANE), f32),
            pltpu.VMEM((3, 4, 2, ROWS, LANE), f32),
            pltpu.VMEM((3, 4, 2, ROWS, LANE), f32),
            pltpu.VMEM((3, 2, ROWS, LANE), f32),
            pltpu.VMEM((3, ROWS, LANE), f32),
            pltpu.VMEM((5, 4, 4, ROWS, LANE), f32),
            pltpu.VMEM((5, 4, 4, ROWS, LANE), f32),
            pltpu.VMEM((5, 4, 4, ROWS, LANE), f32),
            pltpu.VMEM((5, 3, 4, ROWS, LANE), f32),
            pltpu.VMEM((5, 4, ROWS, LANE), f32),
            pltpu.VMEM((5, 4, ROWS, LANE), f32),
            dma(5),
            dma(8), dma(8), dma(8), dma(8), dma(3), dma(3), dma(2, 4), dma(2, 4), dma(2, 4, 3), dma(2, 4, 3), dma(2, 6),
            dma(2, 6), dma(2), dma(2), dma(4, 2), dma(4), dma(2, 4), dma(2, 4), dma(5), dma(5),
            dma(2, 4, 3), dma(2, 4, 3), dma(2, 4, 4), dma(2, 4, 4), dma(1), dma(1),
            pltpu.SemaphoreType.REGULAR, pltpu.SemaphoreType.REGULAR,
        ],
        compiler_params=pltpu.CompilerParams(
            collective_id=0, has_side_effects=True, vmem_limit_bytes=60 * 1024 * 1024
        ),
    )(
        jnp.swapaxes(activations, 0, 1),
        jnp.swapaxes(output_grads, 0, 1),
        old_factors,
        inverses.reshape(ROWS, 1024),
        owners,
    )
    return new_factors, preconditioned.reshape(3, ROWS, 1, LANE)


def solution(mesh):
    placed = (
        P("dp", None, "own"),
        P("dp", None, "own"),
        P(None, "dp", "own"),
        P("own", None, "dp", None),
        P(),
    )
    return jax.shard_map(
        body,
        mesh=mesh,
        in_specs=placed,
        out_specs=(P(None, "dp", "own"), P(None, "dp", None, "own")),
        check_vma=False,
    )
```

```python
import jax
import jax.numpy as jnp
from jax import lax
from jax.experimental import pallas as pl
from jax.experimental.pallas import tpu as pltpu
from jax.sharding import PartitionSpec as P

MESH = pl.DeviceIdType.MESH
FACTOR_DECAY = 0.9
TOKENS = 32768
TOK = 512
PIECES = 4
LANE = 128
ROWS = 16


def gram(lhs8, rhs4, part, j_base, pieces):
    rhs = jnp.concatenate([rhs4[j_base + j] for j in pieces], axis=1)

    def tile(i, _):
        lhs = jnp.concatenate([lhs8[2 * i], lhs8[2 * i + 1]], axis=1)
        out = lax.dot_general(lhs, rhs, (((0,), (0,)), ((), ())), preferred_element_type=jnp.float32)
        for e, j in enumerate(pieces):
            part[j, i] = out[:, e * LANE:(e + 1) * LANE].reshape(4, 2, 2, ROWS, LANE)
        return 0

    lax.fori_loop(0, 4, tile, 0)


def kernel(
    act, grads, old, inv, owners, nf_out, pr_out,
    owner_s, cols, x8, shard, full_inv, s8, a4, old_v, part, half,
    mid_z, near_z, out_z, in_z, sum_z, cross_in,
    y_out, y_in, mid_y, near_y, out_y, in_y,
    loc_sem, xs_sem, xr_sem, is_sem, ir_sem, ns_sem, nr_sem, fs_sem, fr_sem, as_sem, ar_sem, ps_sem, pr_sem,
    ss_sem, sr_sem, bs_sem, br_sem, cs_sem, cr_sem, ys_sem, yr_sem, zs_sem, zr_sem, ws_sem, wr_sem, ts_sem, tr_sem,
    chain_2, chain_4,
):
    dp = lax.axis_index("dp")
    own = lax.axis_index("own")
    z = dp // 4
    k = z // 4
    r = z % 4
    y = (dp // 2) % 2
    c = dp % 2
    h = own // 4
    x = own % 4

    def at(zz, yy, cc, mm):
        return (((zz % 16) * 2 + yy) * 2 + cc, mm)

    def member(hh, xx):
        return (dp, hh * 4 + xx)

    def far(d, xx):
        return at(((k + d) % 4) * 4 + r, y, c, h * 4 + xx)

    core = at(z, y, 1 - c, own)
    across = at(z, 1 - y, c, own)
    diagonal = at(z, 1 - y, 1 - c, own)
    by_z = {d: at(z + d, y, c, own) for d in (1, 15, 2, 14)}
    peers = [((h + d // 4) % 2, (x + d % 4) % 4) for d in range(8)]

    barrier = pltpu.get_barrier_semaphore()
    targets = list(by_z.values()) + [member(*peers[d]) for d in range(1, 8)] + [core, across, diagonal]
    for target in targets:
        pl.semaphore_signal(barrier, inc=1, device_id=target, device_id_type=MESH)
    loc = [
        pltpu.make_async_copy(act, cols.at[pl.ds(0, 1)], loc_sem.at[0]),
        pltpu.make_async_copy(grads, cols.at[pl.ds(1, 3)], loc_sem.at[1]),
        pltpu.make_async_copy(inv.at[:, pl.ds(h * 512, 512)], shard.at[own], loc_sem.at[2]),
        pltpu.make_async_copy(old, old_v, loc_sem.at[3]),
        pltpu.make_async_copy(owners, owner_s, loc_sem.at[4]),
    ]
    for copy in loc:
        copy.start()

    pl.semaphore_wait(barrier, len(targets))
    for d in (2, 14):
        pl.semaphore_signal(chain_2, inc=1, device_id=by_z[d], device_id_type=MESH)

    def remote(src, dst, s_sem, r_sem, target):
        return pltpu.make_async_remote_copy(
            src_ref=src, dst_ref=dst, send_sem=s_sem, recv_sem=r_sem, device_id=target, device_id_type=MESH
        )

    def start(copies):
        for copy in copies:
            copy.start()
        return copies

    inv_copies = start([
        remote(inv.at[:, pl.ds(peers[d][0] * 512, 512)], shard.at[own], is_sem.at[d], ir_sem.at[d], member(*peers[d]))
        for d in (4, 1, 3, 5, 7, 2, 6)
    ])
    pl.semaphore_wait(chain_2, 2)
    for d in (1, 3):
        pl.semaphore_signal(chain_4, inc=1, device_id=far(d, x), device_id_type=MESH)
    loc[2].wait()
    loc[4].wait()
    for copy in inv_copies:
        copy.wait_recv()

    mine = shard[owner_s[x]]
    for u in range(2):
        full_inv[u, k, r, y, c] = mine[:, u * 256:(u + 1) * 256]
    here = full_inv.at[:, k, r, y, c]
    near_copies = start([
        remote(here, here, ns_sem.at[i], nr_sem.at[i], target) for i, target in enumerate((across, diagonal, core))
    ])

    loc[0].wait()
    loc[1].wait()
    x_copies = start([
        remote(cols.at[peers[d][1]], x8.at[own], xs_sem.at[d], xr_sem.at[d], member(*peers[d]))
        for d in (4, 1, 6, 3, 5, 2, 7)
    ])
    x8[own] = cols[x]

    for copy in near_copies:
        copy.wait_recv()

    def far_copy(u, d):
        view = full_inv.at[u, k, r, c]
        return remote(view, view, fs_sem.at[u, d], fr_sem.at[u, d], far(d, x))

    def adj_copy(u, d, i):
        b = (k + d) % 4
        view = full_inv.at[u, b, r, c]
        if i < 2:
            target = by_z[(1, 15)[i]]
        else:
            target = at(z + 2 + (b // 2) * 12, y, c, own)
        return remote(view, view, as_sem.at[u, d, i], ar_sem.at[u, b, i], target)

    def adj_wait(u, i):
        for b in range(4):
            view = full_inv.at[u, b, (r + (3, 1, 2)[i]) % 4, c]
            remote(view, view, as_sem.at[u, 0, i], ar_sem.at[u, b, i], by_z[1]).wait_recv()

    def pass_views(u, cc):
        views = [full_inv.at[u, (k + d) % 4, r, cc] for d in (1, 2, 3)]
        return views + [
            full_inv.at[u, :, (r + 3) % 4, cc], full_inv.at[u, :, (r + 1) % 4, cc], full_inv.at[u, :, (r + 2) % 4, cc],
        ]

    def pass_copy(u, i, cc):
        view = pass_views(u, cc)[i]
        return remote(view, view, ps_sem.at[u, i], pr_sem.at[u, i], core)

    pl.semaphore_wait(chain_4, 2)
    for u in range(2):
        for d in (2, 1, 3):
            far_copy(u, d).start()
    for u in range(2):
        for i in range(3):
            adj_copy(u, 0, i).start()
    for d in (1, 3, 2):
        for u in range(2):
            far_copy(u, d).wait_recv()
            for i in range(3):
                adj_copy(u, 4 - d, i).start()
            pass_copy(u, 3 - d, c).start()

    for copy in x_copies:
        copy.wait_recv()
    gram(x8, x8, part.at[0], h * PIECES, range(PIECES))

    def piece(i):
        return (x + i) % 4

    def core_copy(n, i):
        j = piece(i)
        return remote(part.at[n, j, :, :, :, 1 - c], half.at[n, j], cs_sem.at[n, i], cr_sem.at[n, i], core)

    for i in (3, 0, 1, 2):
        core_copy(0, i).start()

    def z_first(n, i):
        return n == 0 and i < 3

    def slot(n, i):
        return i if z_first(n, i) else i + 1 if n == 1 else 0

    def y_copy(n, i):
        q = slot(n, i)
        return remote(y_out.at[q], y_in.at[q], ys_sem.at[q], yr_sem.at[q], across)

    def y_start(n, i):
        j = piece(i)
        core_copy(n, i).wait_recv()
        y_out[slot(n, i)] = part[n, j, :, :, 1 - y, c] + half[n, j, :, :, 1 - y]
        if n == 1 and i in (3, 0):
            y_copy(n, 1 if i == 3 else 2).wait_send()
        y_copy(n, i).start()

    y_start(0, 3)

    def scale(u):
        for i in range(3):
            adj_wait(u, i)
            pass_copy(u, 3 + i, c).start()
        for i in range(6):
            pass_copy(u, i, 1 - c).wait_recv()
        weights = full_inv[u].reshape(1024, 256)

        def tile(i, _):
            rows = pl.ds(pl.multiple_of(i * 256, 256), 256)
            lhs = jnp.concatenate([x8[m, rows, :] for m in range(8)], axis=1)
            out = jnp.dot(lhs, weights, preferred_element_type=jnp.float32).astype(jnp.bfloat16)
            for j in range(2):
                s8[h * PIECES + 2 * u + j, rows, :] = out[:, j * LANE:(j + 1) * LANE]
            return 0

        lax.fori_loop(0, TOK // 256, tile, 0)

    def swap_copy(u):
        view = s8.at[pl.ds(h * PIECES + 2 * u, 2)]
        return remote(view, view, ss_sem.at[u], sr_sem.at[u], member(1 - h, x))

    def act_copy(j, g):
        return remote(s8.at[h * PIECES + j], a4.at[j], bs_sem.at[j, g // 2], br_sem.at[j], member(h, g))

    def hand_copy(j):
        return remote(a4.at[j], a4.at[j], bs_sem.at[j, 0], br_sem.at[j], member(h, 2))

    def scaled_start(u):
        @pl.when(x == 0)
        def _():
            for i in range(2):
                act_copy(2 * u + i, 1).start()
                act_copy(2 * u + 1 - i, 3).start()

        @pl.when(x > 0)
        def _():
            swap_copy(u).start()

    def hand_on(u):
        for i, g in enumerate((1, 3)):
            @pl.when(x == g)
            def _():
                hand_copy(2 * u + i).wait_recv()
                hand_copy(2 * u + i).start()

    def buffers(n, i):
        return (mid_z, near_z, out_z, in_z) if z_first(n, i) else (mid_y, near_y, out_y, in_y)

    def near_copies_of(n, i):
        mid, near, _, _ = buffers(n, i)
        q = slot(n, i)
        return [
            remote(mid.at[q, :, (r + d) % 4], near.at[q, e], zs_sem.at[n, i, e], zr_sem.at[n, i, e], by_z[d])
            for e, d in enumerate((2 if i % 2 == 0 else 14, 1, 15))
        ]

    def near_start(n, i):
        j, q = piece(i), slot(n, i)
        if z_first(n, i):
            core_copy(n, i).wait_recv()
            mid_z[q] = part[n, j, :, :, :, c] + half[n, j]
        else:
            y_copy(n, i).wait_recv()
            mid_y[q] = part[n, j, :, :, y, c] + half[n, j, :, :, y] + y_in[q]
        start(near_copies_of(n, i))

    def out_copy(n, i, d):
        _, _, out, into = buffers(n, i)
        q = slot(n, i)
        return remote(out.at[q, (k + d) % 4], into.at[q, d], ws_sem.at[n, i, d], wr_sem.at[n, i, d], far(d, piece(i)))

    def outs(i):
        return (2, 1, 3) if i == 0 else (2, 1, 3, 0)

    def out_start(n, i):
        mid, near, out, into = buffers(n, i)
        q = slot(n, i)
        for copy in near_copies_of(n, i):
            copy.wait_recv()
        out[q] = mid[q, :, r] + near[q, 0] + near[q, 1] + near[q, 2]
        for d in outs(i):
            out_copy(n, i, d).start()
        if i == 0:
            into[q, 0] = out[q, k]

    def arrived(n, i):
        into, q = buffers(n, i)[3], slot(n, i)
        for d in outs(i):
            out_copy(n, i, d).wait_recv()
        return into[q, 0] + into[q, 1] + into[q, 2] + into[q, 3]

    def source(i):
        return (x + 4 - i) % 4

    cross_copy = remote(sum_z.at[:, 1 - y], cross_in, ts_sem.at[0], tr_sem.at[0], across)

    def drain(n):
        for i in range(PIECES):
            core_copy(n, i).wait_send()
            for d in outs(i):
                out_copy(n, i, d).wait_send()
            for copy in near_copies_of(n, i):
                copy.wait_send()
        for i in (3, 0)[:1 + n]:
            y_copy(n, i).wait_send()

    scale(0)
    scaled_start(0)
    near_start(0, 0)
    near_start(0, 1)
    scale(1)
    scaled_start(1)
    hand_on(0)
    hand_on(1)
    near_start(0, 2)
    out_start(0, 0)
    near_start(0, 3)
    out_start(0, 1)

    @pl.when(x > 0)
    def _():
        for u in range(2):
            swap_copy(u).wait_recv()
            for i, g in enumerate((1, 3)):
                @pl.when(x != g)
                def _():
                    act_copy(2 * u + i, 1).wait_recv()
        gram(s8, a4, part.at[1], 0, [piece(1), piece(2)])
        core_copy(1, 1).start()
        core_copy(1, 2).start()
        gram(s8, a4, part.at[1], 0, [piece(3), piece(0)])
        y_start(1, 1)
        core_copy(1, 3).start()
        core_copy(1, 0).start()

    out_start(0, 2)

    @pl.when(x > 0)
    def _():
        y_start(1, 2)
        near_start(1, 1)

    out_start(0, 3)

    @pl.when(x > 0)
    def _():
        y_start(1, 3)
        near_start(1, 2)
        y_start(1, 0)
        out_start(1, 1)
        near_start(1, 3)
        out_start(1, 2)
        near_start(1, 0)
        out_start(1, 3)
        out_start(1, 0)

    for i in range(3):
        sum_z[i] = arrived(0, i)
    cross_copy.start()
    loc[3].wait()

    for copy in inv_copies + x_copies + near_copies + [cross_copy]:
        copy.wait_send()
    for u in range(2):
        for d in (1, 2, 3):
            far_copy(u, d).wait_send()
        for d in range(4):
            for i in range(3):
                adj_copy(u, d, i).wait_send()
        for i in range(6):
            pass_copy(u, i, c).wait_send()
    drain(0)

    @pl.when(x == 0)
    def _():
        for j in range(PIECES):
            act_copy(j, 1).wait_send()
            act_copy(j, 3).wait_send()

    for i, g in enumerate((1, 3)):
        @pl.when(x == g)
        def _():
            for u in range(2):
                hand_copy(2 * u + i).wait_send()

    @pl.when(x > 0)
    def _():
        for u in range(2):
            swap_copy(u).wait_send()
        drain(1)


    def factors(i, total):
        b = source(i)
        nf_out[b] = FACTOR_DECAY * old_v[b] + ((1.0 - FACTOR_DECAY) / TOKENS) * total

    factors(3, arrived(0, 3))
    cross_copy.wait_recv()
    for i in range(3):
        factors(i, sum_z[i, y] + cross_in[i])

    for i in (1, 2, 3, 0):
        @pl.when(source(i) > 0)
        def _():
            pr_out[source(i) - 1] = arrived(1, i) * (1.0 / TOKENS)


def body(activations, output_grads, old_factors, inverses, owners):
    vmem = pl.BlockSpec(memory_space=pltpu.VMEM)
    hbm = pl.BlockSpec(memory_space=pl.ANY)
    bf16, f32 = jnp.bfloat16, jnp.float32
    dma = lambda *shape: pltpu.SemaphoreType.DMA(shape)
    new_factors, preconditioned = pl.pallas_call(
        kernel,
        out_shape=(
            jax.ShapeDtypeStruct((4, ROWS, LANE), f32),
            jax.ShapeDtypeStruct((3, ROWS, LANE), f32),
        ),
        in_specs=[hbm, hbm, hbm, hbm, hbm],
        out_specs=(vmem, vmem),
        scratch_shapes=[
            pltpu.SMEM((4,), jnp.int32),
            pltpu.VMEM((4, TOK, LANE), bf16),
            pltpu.VMEM((8, TOK, LANE), bf16),
            pltpu.VMEM((8, ROWS, 512), bf16),
            pltpu.VMEM((2, 4, 4, 2, 2, ROWS, 256), bf16),
            pltpu.VMEM((8, TOK, LANE), bf16),
            pltpu.VMEM((4, TOK, LANE), bf16),
            pltpu.VMEM((4, ROWS, LANE), f32),
            pltpu.VMEM((2, PIECES, 4, 4, 2, 2, ROWS, LANE), f32),
            pltpu.VMEM((2, PIECES, 4, 4, 2, ROWS, LANE), f32),
            pltpu.VMEM((3, 4, 4, 2, ROWS, LANE), f32),
            pltpu.VMEM((3, 3, 4, 2, ROWS, LANE), f32),
            pltpu.VMEM((3, 4, 2, ROWS, LANE), f32),
            pltpu.VMEM((3, 4, 2, ROWS, LANE), f32),
            pltpu.VMEM((3, 2, ROWS, LANE), f32),
            pltpu.VMEM((3, ROWS, LANE), f32),
            pltpu.VMEM((5, 4, 4, ROWS, LANE), f32),
            pltpu.VMEM((5, 4, 4, ROWS, LANE), f32),
            pltpu.VMEM((5, 4, 4, ROWS, LANE), f32),
            pltpu.VMEM((5, 3, 4, ROWS, LANE), f32),
            pltpu.VMEM((5, 4, ROWS, LANE), f32),
            pltpu.VMEM((5, 4, ROWS, LANE), f32),
            dma(5),
            dma(8), dma(8), dma(8), dma(8), dma(3), dma(3), dma(2, 4), dma(2, 4), dma(2, 4, 3), dma(2, 4, 3), dma(2, 6),
            dma(2, 6), dma(2), dma(2), dma(4, 2), dma(4), dma(2, 4), dma(2, 4), dma(5), dma(5),
            dma(2, 4, 3), dma(2, 4, 3), dma(2, 4, 4), dma(2, 4, 4), dma(1), dma(1),
            pltpu.SemaphoreType.REGULAR, pltpu.SemaphoreType.REGULAR,
        ],
        compiler_params=pltpu.CompilerParams(
            collective_id=0, has_side_effects=True, vmem_limit_bytes=60 * 1024 * 1024
        ),
    )(
        jnp.swapaxes(activations, 0, 1),
        jnp.swapaxes(output_grads, 0, 1),
        old_factors,
        inverses.reshape(ROWS, 1024),
        owners,
    )
    return new_factors, preconditioned.reshape(3, ROWS, 1, LANE)


def solution(mesh):
    placed = (
        P("dp", None, "own"),
        P("dp", None, "own"),
        P(None, "dp", "own"),
        P("own", None, "dp", None),
        P(),
    )
    return jax.shard_map(
        body,
        mesh=mesh,
        in_specs=placed,
        out_specs=(P(None, "dp", "own"), P(None, "dp", None, "own")),
        check_vma=False,
    )
```

```python
import jax
import jax.numpy as jnp
from jax import lax
from jax.experimental import pallas as pl
from jax.experimental.pallas import tpu as pltpu
from jax.sharding import PartitionSpec as P

MESH = pl.DeviceIdType.MESH
FACTOR_DECAY = 0.9
TOKENS = 32768
TOK = 512
PIECES = 4
LANE = 128
ROWS = 16


def gram(lhs8, rhs4, part, j_base, pieces):
    rhs = jnp.concatenate([rhs4[j_base + j] for j in pieces], axis=1)

    def tile(i, _):
        lhs = jnp.concatenate([lhs8[2 * i], lhs8[2 * i + 1]], axis=1)
        out = lax.dot_general(lhs, rhs, (((0,), (0,)), ((), ())), preferred_element_type=jnp.float32)
        for e, j in enumerate(pieces):
            part[j, i] = out[:, e * LANE:(e + 1) * LANE].reshape(4, 2, 2, ROWS, LANE)
        return 0

    lax.fori_loop(0, 4, tile, 0)


def kernel(
    act, grads, old, inv, owners, nf_hbm, pr_hbm, nf_out, pr_out,
    owner_s, cols, x8, shard, full_inv, s8, a4, old_v, part, half,
    mid_z, near_z, out_z, in_z, sum_z, cross_in,
    y_out, y_in, mid_y, near_y, out_y, in_y,
    loc_sem, xs_sem, xr_sem, is_sem, ir_sem, ns_sem, nr_sem, fs_sem, fr_sem, as_sem, ar_sem, ps_sem, pr_sem,
    ss_sem, sr_sem, bs_sem, br_sem, cs_sem, cr_sem, ys_sem, yr_sem, zs_sem, zr_sem, ws_sem, wr_sem, ts_sem, tr_sem,
    chain_2, chain_4,
):
    dp = lax.axis_index("dp")
    own = lax.axis_index("own")
    z = dp // 4
    k = z // 4
    r = z % 4
    y = (dp // 2) % 2
    c = dp % 2
    h = own // 4
    x = own % 4

    def at(zz, yy, cc, mm):
        return (((zz % 16) * 2 + yy) * 2 + cc, mm)

    def member(hh, xx):
        return (dp, hh * 4 + xx)

    def far(d, xx):
        return at(((k + d) % 4) * 4 + r, y, c, h * 4 + xx)

    core = at(z, y, 1 - c, own)
    across = at(z, 1 - y, c, own)
    diagonal = at(z, 1 - y, 1 - c, own)
    by_z = {d: at(z + d, y, c, own) for d in (1, 15, 2, 14)}
    peers = [((h + d // 4) % 2, (x + d % 4) % 4) for d in range(8)]

    barrier = pltpu.get_barrier_semaphore()
    targets = list(by_z.values()) + [member(*peers[d]) for d in range(1, 8)] + [core, across, diagonal]
    for target in targets:
        pl.semaphore_signal(barrier, inc=1, device_id=target, device_id_type=MESH)
    loc = [
        pltpu.make_async_copy(act, cols.at[pl.ds(0, 1)], loc_sem.at[0]),
        pltpu.make_async_copy(grads, cols.at[pl.ds(1, 3)], loc_sem.at[1]),
        pltpu.make_async_copy(inv.at[:, pl.ds(h * 512, 512)], shard.at[own], loc_sem.at[2]),
        pltpu.make_async_copy(old, old_v, loc_sem.at[3]),
        pltpu.make_async_copy(owners, owner_s, loc_sem.at[4]),
    ]
    for copy in loc:
        copy.start()

    pl.semaphore_wait(barrier, len(targets))
    for d in (2, 14):
        pl.semaphore_signal(chain_2, inc=1, device_id=by_z[d], device_id_type=MESH)

    def remote(src, dst, s_sem, r_sem, target):
        return pltpu.make_async_remote_copy(
            src_ref=src, dst_ref=dst, send_sem=s_sem, recv_sem=r_sem, device_id=target, device_id_type=MESH
        )

    def start(copies):
        for copy in copies:
            copy.start()
        return copies

    inv_copies = start([
        remote(inv.at[:, pl.ds(peers[d][0] * 512, 512)], shard.at[own], is_sem.at[d], ir_sem.at[d], member(*peers[d]))
        for d in (4, 1, 3, 5, 7, 2, 6)
    ])
    pl.semaphore_wait(chain_2, 2)
    for d in (1, 3):
        pl.semaphore_signal(chain_4, inc=1, device_id=far(d, x), device_id_type=MESH)
    loc[2].wait()
    loc[4].wait()
    for copy in inv_copies:
        copy.wait_recv()

    mine = shard[owner_s[x]]
    for u in range(2):
        full_inv[u, k, r, y, c] = mine[:, u * 256:(u + 1) * 256]
    here = full_inv.at[:, k, r, y, c]
    near_copies = start([
        remote(here, here, ns_sem.at[i], nr_sem.at[i], target) for i, target in enumerate((across, diagonal, core))
    ])

    loc[0].wait()
    loc[1].wait()
    x_copies = start([
        remote(cols.at[peers[d][1]], x8.at[own], xs_sem.at[d], xr_sem.at[d], member(*peers[d]))
        for d in (4, 1, 6, 3, 5, 2, 7)
    ])
    x8[own] = cols[x]

    for copy in near_copies:
        copy.wait_recv()

    def far_copy(u, d):
        view = full_inv.at[u, k, r, c]
        return remote(view, view, fs_sem.at[u, d], fr_sem.at[u, d], far(d, x))

    def adj_copy(u, d, i):
        b = (k + d) % 4
        view = full_inv.at[u, b, r, c]
        if i < 2:
            target = by_z[(1, 15)[i]]
        else:
            target = at(z + 2 + (b // 2) * 12, y, c, own)
        return remote(view, view, as_sem.at[u, d, i], ar_sem.at[u, b, i], target)

    def adj_wait(u, i):
        for b in range(4):
            view = full_inv.at[u, b, (r + (3, 1, 2)[i]) % 4, c]
            remote(view, view, as_sem.at[u, 0, i], ar_sem.at[u, b, i], by_z[1]).wait_recv()

    def pass_views(u, cc):
        views = [full_inv.at[u, (k + d) % 4, r, cc] for d in (1, 2, 3)]
        return views + [
            full_inv.at[u, :, (r + 3) % 4, cc], full_inv.at[u, :, (r + 1) % 4, cc], full_inv.at[u, :, (r + 2) % 4, cc],
        ]

    def pass_copy(u, i, cc):
        view = pass_views(u, cc)[i]
        return remote(view, view, ps_sem.at[u, i], pr_sem.at[u, i], core)

    pl.semaphore_wait(chain_4, 2)
    for u in range(2):
        for d in (2, 1, 3):
            far_copy(u, d).start()
    for u in range(2):
        for i in range(3):
            adj_copy(u, 0, i).start()
    for d in (1, 3, 2):
        for u in range(2):
            far_copy(u, d).wait_recv()
            for i in range(3):
                adj_copy(u, 4 - d, i).start()
            pass_copy(u, 3 - d, c).start()

    for copy in x_copies:
        copy.wait_recv()
    gram(x8, x8, part.at[0], h * PIECES, range(PIECES))

    def piece(i):
        return (x + i) % 4

    def core_copy(n, i):
        j = piece(i)
        return remote(part.at[n, j, :, :, :, 1 - c], half.at[n, j], cs_sem.at[n, i], cr_sem.at[n, i], core)

    for i in (3, 0, 1, 2):
        core_copy(0, i).start()

    def z_first(n, i):
        return n == 0 and i < 3

    def slot(n, i):
        return i if z_first(n, i) else i + 1 if n == 1 else 0

    def y_copy(n, i):
        q = slot(n, i)
        return remote(y_out.at[q], y_in.at[q], ys_sem.at[q], yr_sem.at[q], across)

    def y_start(n, i):
        j = piece(i)
        core_copy(n, i).wait_recv()
        y_out[slot(n, i)] = part[n, j, :, :, 1 - y, c] + half[n, j, :, :, 1 - y]
        if n == 1 and i in (3, 0):
            y_copy(n, 1 if i == 3 else 2).wait_send()
        y_copy(n, i).start()

    y_start(0, 3)

    def scale(u):
        for i in range(3):
            adj_wait(u, i)
            pass_copy(u, 3 + i, c).start()
        for i in range(6):
            pass_copy(u, i, 1 - c).wait_recv()
        weights = full_inv[u].reshape(1024, 256)

        def tile(i, _):
            rows = pl.ds(pl.multiple_of(i * 256, 256), 256)
            lhs = jnp.concatenate([x8[m, rows, :] for m in range(8)], axis=1)
            out = jnp.dot(lhs, weights, preferred_element_type=jnp.float32).astype(jnp.bfloat16)
            for j in range(2):
                s8[h * PIECES + 2 * u + j, rows, :] = out[:, j * LANE:(j + 1) * LANE]
            return 0

        lax.fori_loop(0, TOK // 256, tile, 0)

    def swap_copy(u):
        view = s8.at[pl.ds(h * PIECES + 2 * u, 2)]
        return remote(view, view, ss_sem.at[u], sr_sem.at[u], member(1 - h, x))

    def act_copy(j, g):
        return remote(s8.at[h * PIECES + j], a4.at[j], bs_sem.at[j, g // 2], br_sem.at[j], member(h, g))

    def hand_copy(j):
        return remote(a4.at[j], a4.at[j], bs_sem.at[j, 0], br_sem.at[j], member(h, 2))

    def scaled_start(u):
        @pl.when(x == 0)
        def _():
            for i in range(2):
                act_copy(2 * u + i, 1).start()
                act_copy(2 * u + 1 - i, 3).start()

        @pl.when(x > 0)
        def _():
            swap_copy(u).start()

    def hand_on(u):
        for i, g in enumerate((1, 3)):
            @pl.when(x == g)
            def _():
                hand_copy(2 * u + i).wait_recv()
                hand_copy(2 * u + i).start()

    def buffers(n, i):
        return (mid_z, near_z, out_z, in_z) if z_first(n, i) else (mid_y, near_y, out_y, in_y)

    def near_copies_of(n, i):
        mid, near, _, _ = buffers(n, i)
        q = slot(n, i)
        return [
            remote(mid.at[q, :, (r + d) % 4], near.at[q, e], zs_sem.at[n, i, e], zr_sem.at[n, i, e], by_z[d])
            for e, d in enumerate((2 if i % 2 == 0 else 14, 1, 15))
        ]

    def near_start(n, i):
        j, q = piece(i), slot(n, i)
        if z_first(n, i):
            core_copy(n, i).wait_recv()
            mid_z[q] = part[n, j, :, :, :, c] + half[n, j]
        else:
            y_copy(n, i).wait_recv()
            mid_y[q] = part[n, j, :, :, y, c] + half[n, j, :, :, y] + y_in[q]
        start(near_copies_of(n, i))

    def out_copy(n, i, d):
        _, _, out, into = buffers(n, i)
        q = slot(n, i)
        return remote(out.at[q, (k + d) % 4], into.at[q, d], ws_sem.at[n, i, d], wr_sem.at[n, i, d], far(d, piece(i)))

    def outs(i):
        return (2, 1, 3) if i == 0 else (2, 1, 3, 0)

    def out_start(n, i):
        mid, near, out, into = buffers(n, i)
        q = slot(n, i)
        for copy in near_copies_of(n, i):
            copy.wait_recv()
        out[q] = mid[q, :, r] + near[q, 0] + near[q, 1] + near[q, 2]
        for d in outs(i):
            out_copy(n, i, d).start()
        if i == 0:
            into[q, 0] = out[q, k]

    def arrived(n, i):
        into, q = buffers(n, i)[3], slot(n, i)
        for d in outs(i):
            out_copy(n, i, d).wait_recv()
        return into[q, 0] + into[q, 1] + into[q, 2] + into[q, 3]

    def source(i):
        return (x + 4 - i) % 4

    cross_copy = remote(sum_z.at[:, 1 - y], cross_in, ts_sem.at[0], tr_sem.at[0], across)

    def drain(n):
        for i in range(PIECES):
            core_copy(n, i).wait_send()
            for d in outs(i):
                out_copy(n, i, d).wait_send()
            for copy in near_copies_of(n, i):
                copy.wait_send()
        for i in (3, 0)[:1 + n]:
            y_copy(n, i).wait_send()

    scale(0)
    scaled_start(0)
    near_start(0, 0)
    near_start(0, 1)
    scale(1)
    scaled_start(1)
    hand_on(0)
    hand_on(1)
    near_start(0, 2)
    out_start(0, 0)
    near_start(0, 3)
    out_start(0, 1)

    @pl.when(x > 0)
    def _():
        for u in range(2):
            swap_copy(u).wait_recv()
            for i, g in enumerate((1, 3)):
                @pl.when(x != g)
                def _():
                    act_copy(2 * u + i, 1).wait_recv()
        gram(s8, a4, part.at[1], 0, [piece(1), piece(2)])
        core_copy(1, 1).start()
        core_copy(1, 2).start()
        gram(s8, a4, part.at[1], 0, [piece(3), piece(0)])
        y_start(1, 1)
        core_copy(1, 3).start()
        core_copy(1, 0).start()

    out_start(0, 2)

    @pl.when(x > 0)
    def _():
        y_start(1, 2)
        near_start(1, 1)

    out_start(0, 3)

    @pl.when(x > 0)
    def _():
        y_start(1, 3)
        near_start(1, 2)
        y_start(1, 0)
        out_start(1, 1)
        near_start(1, 3)
        out_start(1, 2)
        near_start(1, 0)
        out_start(1, 3)
        out_start(1, 0)

    for i in range(3):
        sum_z[i] = arrived(0, i)
    cross_copy.start()
    loc[3].wait()

    for copy in inv_copies + x_copies + near_copies + [cross_copy]:
        copy.wait_send()
    for u in range(2):
        for d in (1, 2, 3):
            far_copy(u, d).wait_send()
        for d in range(4):
            for i in range(3):
                adj_copy(u, d, i).wait_send()
        for i in range(6):
            pass_copy(u, i, c).wait_send()
    drain(0)

    @pl.when(x == 0)
    def _():
        for j in range(PIECES):
            act_copy(j, 1).wait_send()
            act_copy(j, 3).wait_send()

    for i, g in enumerate((1, 3)):
        @pl.when(x == g)
        def _():
            for u in range(2):
                hand_copy(2 * u + i).wait_send()

    @pl.when(x > 0)
    def _():
        for u in range(2):
            swap_copy(u).wait_send()
        drain(1)


    def factors(i, total):
        b = source(i)
        nf_out[b] = FACTOR_DECAY * old_v[b] + ((1.0 - FACTOR_DECAY) / TOKENS) * total

    factors(3, arrived(0, 3))
    cross_copy.wait_recv()
    for i in range(3):
        factors(i, sum_z[i, y] + cross_in[i])

    nf_copy = pltpu.make_async_copy(nf_out, nf_hbm, loc_sem.at[5])
    nf_copy.start()

    for i in (1, 2, 3, 0):
        @pl.when(source(i) > 0)
        def _():
            pr_out[source(i) - 1] = arrived(1, i) * (1.0 / TOKENS)

    pr_copy = pltpu.make_async_copy(pr_out, pr_hbm, loc_sem.at[6])
    pr_copy.start()
    nf_copy.wait()
    pr_copy.wait()


def body(activations, output_grads, old_factors, inverses, owners):
    hbm = pl.BlockSpec(memory_space=pl.ANY)
    bf16, f32 = jnp.bfloat16, jnp.float32
    dma = lambda *shape: pltpu.SemaphoreType.DMA(shape)
    new_factors, preconditioned = pl.pallas_call(
        kernel,
        out_shape=(
            jax.ShapeDtypeStruct((4, ROWS, LANE), f32),
            jax.ShapeDtypeStruct((3, ROWS, LANE), f32),
        ),
        in_specs=[hbm, hbm, hbm, hbm, hbm],
        out_specs=(hbm, hbm),
        scratch_shapes=[
            pltpu.VMEM((4, ROWS, LANE), f32),
            pltpu.VMEM((3, ROWS, LANE), f32),
            pltpu.SMEM((4,), jnp.int32),
            pltpu.VMEM((4, TOK, LANE), bf16),
            pltpu.VMEM((8, TOK, LANE), bf16),
            pltpu.VMEM((8, ROWS, 512), bf16),
            pltpu.VMEM((2, 4, 4, 2, 2, ROWS, 256), bf16),
            pltpu.VMEM((8, TOK, LANE), bf16),
            pltpu.VMEM((4, TOK, LANE), bf16),
            pltpu.VMEM((4, ROWS, LANE), f32),
            pltpu.VMEM((2, PIECES, 4, 4, 2, 2, ROWS, LANE), f32),
            pltpu.VMEM((2, PIECES, 4, 4, 2, ROWS, LANE), f32),
            pltpu.VMEM((3, 4, 4, 2, ROWS, LANE), f32),
            pltpu.VMEM((3, 3, 4, 2, ROWS, LANE), f32),
            pltpu.VMEM((3, 4, 2, ROWS, LANE), f32),
            pltpu.VMEM((3, 4, 2, ROWS, LANE), f32),
            pltpu.VMEM((3, 2, ROWS, LANE), f32),
            pltpu.VMEM((3, ROWS, LANE), f32),
            pltpu.VMEM((5, 4, 4, ROWS, LANE), f32),
            pltpu.VMEM((5, 4, 4, ROWS, LANE), f32),
            pltpu.VMEM((5, 4, 4, ROWS, LANE), f32),
            pltpu.VMEM((5, 3, 4, ROWS, LANE), f32),
            pltpu.VMEM((5, 4, ROWS, LANE), f32),
            pltpu.VMEM((5, 4, ROWS, LANE), f32),
            dma(7),
            dma(8), dma(8), dma(8), dma(8), dma(3), dma(3), dma(2, 4), dma(2, 4), dma(2, 4, 3), dma(2, 4, 3), dma(2, 6),
            dma(2, 6), dma(2), dma(2), dma(4, 2), dma(4), dma(2, 4), dma(2, 4), dma(5), dma(5),
            dma(2, 4, 3), dma(2, 4, 3), dma(2, 4, 4), dma(2, 4, 4), dma(1), dma(1),
            pltpu.SemaphoreType.REGULAR, pltpu.SemaphoreType.REGULAR,
        ],
        compiler_params=pltpu.CompilerParams(
            collective_id=0, has_side_effects=True, vmem_limit_bytes=60 * 1024 * 1024
        ),
    )(
        jnp.swapaxes(activations, 0, 1),
        jnp.swapaxes(output_grads, 0, 1),
        old_factors,
        inverses.reshape(ROWS, 1024),
        owners,
    )
    return new_factors, preconditioned.reshape(3, ROWS, 1, LANE)


def solution(mesh):
    placed = (
        P("dp", None, "own"),
        P("dp", None, "own"),
        P(None, "dp", "own"),
        P("own", None, "dp", None),
        P(),
    )
    return jax.shard_map(
        body,
        mesh=mesh,
        in_specs=placed,
        out_specs=(P(None, "dp", "own"), P(None, "dp", None, "own")),
        check_vma=False,
    )
```
